32 devices in a mesh: seq: 8 (over z, y), head: 4 (over x, core).
Axes of the slice: x: 2, y: 2, z: 4, core: 2. Of those that a mesh axis runs over, the one named last changes fastest.
Arguments:
- queries: bfloat16 [4096, 64, 128], P(('seq', 'head')), may hold values from -6 to 6
- key_heads: bfloat16 [4096, 64, 128], P(('seq', 'head')), may hold values from -6 to 6
- value_heads: bfloat16 [4096, 64, 128], P(('seq', 'head')), may hold values from -6 to 6
- grad_output: bfloat16 [4096, 64, 128], P(('seq', 'head')), may hold values from -6 to 6
- doc_lengths: int32 [16], replicated, may hold values from 1 to 2048, 4096 in all
Outputs:
- query_gradient: bfloat16 [4096, 64, 128], P(('seq', 'head'))
- lookup_derivative: bfloat16 [4096, 64, 128], P(('seq', 'head'))
- content_derivative: bfloat16 [4096, 64, 128], P(('seq', 'head'))
The draws below stay inside these ranges and needn't reach their ends.
Inputs may be any that keep to these rules, and one draw needn't show every extreme that they name: `doc_lengths`: the lengths sum to 4096; the longest is exactly 2048.
All inputs are finite; a program needn't handle non-finite values.
Results may differ from the reference program's by a relative error of at most 0.005.
Values may be sent and summed in bfloat16 or wider, within the bound.
No kernel may reach another device: no remote copies, remote signals or barrier semaphores. Data moves between devices by JAX's collectives and lax.ppermute only.
A program may use at most 128 MiB of HBM per device.

```python
import math
import jax
import jax.numpy as jnp
import numpy as np
from jax import lax

H = 64
HD = 128
BLOCK = 256
NDOC = 16
TOKENS = 4096


def steps_of(stream_key, extent, shards, smallest, high):
    gain, own = 1.0, jax.random.fold_in(stream_key, 6)
    for axis_at, blocks in shards:
        heights = jnp.exp(jax.random.uniform(jax.random.fold_in(own, axis_at), (blocks,), jnp.float32, smallest / len(shards), high / len(shards)))
        gain = gain * jnp.repeat(heights, extent[axis_at] // blocks).reshape([-1 if axis == axis_at else 1 for axis in range(len(extent))])
    return gain


def length_profile(amount, total, limit, slope):
    portions = [(1 << 20) // math.isqrt(standing ** slope) + 1 for standing in range(2, amount + 1)]
    surplus, counts = total - limit - (amount - 1), [1] * (amount - 1)
    while surplus > 0:
        candidates = [i for i in range(amount - 1) if counts[i] < limit]
        whole, budget = sum([portions[i] for i in candidates]), surplus
        for i in candidates:
            addition = min(limit - counts[i], max(1, budget * portions[i] // whole), surplus)
            counts[i] = counts[i] + addition
            surplus = surplus - addition
    return np.array([limit] + counts)


def ragged_sizes(own_key, amount, total, bound, skew):
    if amount == 2:
        one = jax.random.randint(own_key, (), max(1, total - bound), min(bound, total - 1) + 1)
        return jnp.stack([one, total - one])
    sizes = jnp.asarray(length_profile(amount, total, bound, skew), jnp.int32)
    pairs = (amount - 1) // 2
    source_of, receiver = sizes[1:1 + 2 * pairs:2], sizes[2:2 + 2 * pairs:2]
    margin = jnp.minimum(source_of - 1, bound - receiver)
    shifted = jax.random.randint(jax.random.fold_in(own_key, 1), (pairs,), 0, 1 << 20) % (margin + 1)
    sizes = sizes.at[1:1 + 2 * pairs:2].set(source_of - shifted).at[2:2 + 2 * pairs:2].set(receiver + shifted)
    return sizes[jax.random.permutation(jax.random.fold_in(own_key, 2), amount)]


def noise(key, extent, width, reach, shards=(), kind=jnp.bfloat16):
    drawn = width * jax.random.normal(key, extent, jnp.float32)
    if shards:
        drawn = drawn * steps_of(key, extent, shards, -0.22, 0.18)
    return jnp.clip(drawn, -reach, reach).astype(kind)


def setup_inputs(seed: int = 0) -> dict:
    splits = jax.random.split(jax.random.key(seed), 6)
    return {
        "queries": noise(splits[0], (TOKENS, H, HD), 1.0, 6.0, ((0, 32),)),
        "key_heads": noise(splits[1], (TOKENS, H, HD), 1.0, 6.0, ((0, 32),)),
        "value_heads": noise(splits[2], (TOKENS, H, HD), 1.0, 6.0, ((0, 32),)),
        "grad_output": noise(splits[3], (TOKENS, H, HD), 1.0, 6.0, ((0, 32),)),
        "doc_lengths": ragged_sizes(splits[4], NDOC, TOKENS, TOKENS // 2, 2).astype(jnp.int32),
    }


def doc_index(doc_lengths, positions):
    ends = jnp.cumsum(doc_lengths).astype(jnp.int32)
    return lax.optimization_barrier(jnp.sum((ends[None, :] <= positions[:, None]).astype(jnp.int32), axis=1)).astype(jnp.int32)

def reference(queries, key_heads, value_heads, grad_output, doc_lengths):
    tokens_all, head_count, head_width = queries.shape
    scaling = 1.0 / math.sqrt(head_width * (tokens_all // 2))
    blocks = tokens_all // BLOCK
    doc_of = doc_index(doc_lengths, jnp.arange(tokens_all, dtype=jnp.int32)).reshape(blocks, BLOCK)

    def split_blocks(array):
        return array.reshape(blocks, BLOCK, head_count, head_width)
    query_blocks = split_blocks(queries)
    key_blocks = split_blocks(key_heads)
    value_blocks = split_blocks(value_heads)
    grad_blocks = split_blocks(grad_output)
    zero_state = jnp.zeros((head_count, head_width, head_width), jnp.float32)
    row_ids = jnp.arange(BLOCK, dtype=jnp.int32)
    causal = row_ids[:, None] >= row_ids[None, :]

    def backward_step(carried, inputs):
        running, next_doc = carried
        query_rows, grad_rows, block_docs = inputs
        state_in = jnp.where(block_docs[-1] == next_doc, running, jnp.float32(0.0))
        first_rows = (block_docs == block_docs[0]).astype(jnp.float32)
        within_block_sum = jnp.einsum('thq,thv->hqv', query_rows.astype(jnp.float32) * first_rows[:, None, None], grad_rows.astype(jnp.float32))
        running = jnp.where(block_docs[0] == next_doc, running, jnp.float32(0.0)) + within_block_sum
        return ((running, block_docs[0]), (scaling * state_in).astype(jnp.bfloat16))
    _, suffix = lax.scan(backward_step, (zero_state, jnp.int32(-1)), (query_blocks, grad_blocks, doc_of), reverse=True)

    def forward_step(carried, inputs):
        running, prev_doc = carried
        query_rows, key_rows, value_rows, grad_rows, block_docs, other_memory = inputs
        state_in = jnp.where(block_docs[0] == prev_doc, running, jnp.float32(0.0))
        first_state = lax.optimization_barrier((scaling * state_in).astype(jnp.bfloat16)).astype(jnp.float32)
        other_memory = lax.optimization_barrier(other_memory).astype(jnp.float32)
        probe_f32 = query_rows.astype(jnp.float32)
        lookup_alone = key_rows.astype(jnp.float32)
        content_alone = value_rows.astype(jnp.float32)
        derivative_alone = grad_rows.astype(jnp.float32)
        same_doc = ((block_docs[:, None] == block_docs[None, :]) & causal).astype(jnp.float32)
        affinity_derivative = jnp.einsum('thd,shd->hts', derivative_alone, content_alone) * scaling * same_doc[None]
        affinity_derivative = lax.optimization_barrier(affinity_derivative.astype(jnp.bfloat16)).astype(jnp.float32)
        affinity_table = jnp.einsum('thd,shd->hts', probe_f32, lookup_alone) * scaling * same_doc[None]
        affinity_table = lax.optimization_barrier(affinity_table.astype(jnp.bfloat16)).astype(jnp.float32)
        leading_head_rows = (block_docs == block_docs[0]).astype(jnp.float32)[:, None, None]
        remaining_lines = (block_docs == block_docs[-1]).astype(jnp.float32)[:, None, None]
        query_gradient = jnp.einsum('lca,alg->clg', affinity_derivative, lookup_alone) + jnp.einsum('dgj,gsj->dgs', derivative_alone * leading_head_rows, first_state)
        lookup_derivative = jnp.einsum('gjh,jgt->hgt', affinity_derivative, probe_f32) + jnp.einsum('lcg,cng->lcn', content_alone * remaining_lines, other_memory)
        content_derivative = jnp.einsum('gjh,jgt->hgt', affinity_table, derivative_alone) + jnp.einsum('qpf,pfe->qpe', lookup_alone * remaining_lines, other_memory)
        final_rows = (block_docs == block_docs[-1]).astype(jnp.float32)
        within_block_sum = jnp.einsum('icy,icf->cyf', lookup_alone * final_rows[:, None, None], content_alone)
        running = jnp.where(block_docs[-1] == prev_doc, running, jnp.float32(0.0)) + within_block_sum
        return ((running, block_docs[-1]), (query_gradient.astype(jnp.bfloat16), lookup_derivative.astype(jnp.bfloat16), content_derivative.astype(jnp.bfloat16)))
    _, (query_gradient, lookup_derivative, content_derivative) = lax.scan(forward_step, (zero_state, jnp.int32(-1)), (query_blocks, key_blocks, value_blocks, grad_blocks, doc_of, suffix))
    shape = (tokens_all, head_count, head_width)
    return (query_gradient.reshape(shape), lookup_derivative.reshape(shape), content_derivative.reshape(shape))
```

```python
import functools
import math

import jax
import jax.numpy as jnp
from jax import lax
from jax.experimental import pallas as pl
from jax.experimental.pallas import tpu as pltpu
from jax.sharding import PartitionSpec as P

CHUNKS = 4
VMEM = 48 * 1024 * 1024


def _log2(n):
    k = n.bit_length() - 1
    assert 1 << k == n
    return k


def _edges(len_ref, first, last):
    start, stop, total = jnp.int32(0), None, jnp.int32(0)
    big = jnp.int32(2**30)
    stop = big
    for k in range(len_ref.shape[0]):
        total = total + len_ref[k]
        start = jnp.where(total <= last, jnp.maximum(start, total), start)
        stop = jnp.where(total > first, jnp.minimum(stop, total), stop)
    return start, stop


def _dot(a, b, ca, cb):
    return lax.dot_general(
        a, b, (((ca,), (cb,)), ((), ())), preferred_element_type=jnp.float32
    )


def states_kernel(
    place_ref, len_ref, q_ref, k_ref, v_ref, g_ref, keep_ref, send_ref, qs, ks, vs, gs
):
    n, heads, d = q_ref.shape
    first = place_ref[0] * n
    flip = place_ref[1]
    start, stop = _edges(len_ref, first, first + n - 1)
    row = lax.broadcasted_iota(jnp.int32, (n, d), 0) + first
    in_last = row >= start
    in_first = row < stop
    for ref, scr in ((q_ref, qs), (k_ref, ks), (v_ref, vs), (g_ref, gs)):
        scr[...] = ref[...].astype(jnp.float32).reshape(n * heads, d)
    for r in range(heads):
        at = pl.ds(r ^ flip, n, stride=heads)
        out, o = (keep_ref, r) if r < heads // 2 else (send_ref, r - heads // 2)
        key = jnp.where(in_last, ks[at, :], 0.0).astype(jnp.bfloat16)
        value = vs[at, :].astype(jnp.bfloat16)
        out[0, o] = _dot(value, key, 0, 0).astype(out.dtype)
        query = jnp.where(in_first, qs[at, :], 0.0).astype(jnp.bfloat16)
        grad = gs[at, :].astype(jnp.bfloat16)
        out[1, o] = _dot(query, grad, 0, 0).astype(out.dtype)


def grads_kernel(
    scaling,
    place_ref,
    len_ref,
    q_ref,
    k_ref,
    v_ref,
    g_ref,
    mine_ref,
    got_ref,
    *rest,
):
    dq_ref, dk_ref, dv_ref, qs, ks, vs, gs, dqs, dks, dvs = rest[-10:]
    n, heads, d = q_ref.shape
    first = place_ref[0] * n
    flip = place_ref[1]
    start, stop = _edges(len_ref, first, first + n - 1)
    row = lax.broadcasted_iota(jnp.int32, (n, d), 0) + first
    in_last = row >= start
    in_first = row < stop
    t = lax.broadcasted_iota(jnp.int32, (n, n), 0) + first
    s = lax.broadcasted_iota(jnp.int32, (n, n), 1) + first
    begin = jnp.zeros((n, n), jnp.int32)
    total = jnp.int32(0)
    for k in range(len_ref.shape[0]):
        total = total + len_ref[k]
        begin = jnp.where(t >= total, total, begin)
    weight = jnp.where((s <= t) & (s >= begin), jnp.float32(scaling), jnp.float32(0.0))
    for ref, scr in ((q_ref, qs), (k_ref, ks), (v_ref, vs), (g_ref, gs)):
        scr[...] = ref[...].astype(jnp.float32).reshape(n * heads, d)
    for r in range(heads):
        at = pl.ds(r ^ flip, n, stride=heads)
        ref, o = (mine_ref, r) if r < heads // 2 else (got_ref, r - heads // 2)
        state_a = ref[0, o]
        state_b = ref[1, o]
        kf, vf, gf = ks[at, :], vs[at, :], gs[at, :]
        query = qs[at, :].astype(jnp.bfloat16)
        key = kf.astype(jnp.bfloat16)
        value = vf.astype(jnp.bfloat16)
        grad = gf.astype(jnp.bfloat16)
        grad_first = jnp.where(in_first, gf, 0.0).astype(jnp.bfloat16)
        value_last = jnp.where(in_last, vf, 0.0).astype(jnp.bfloat16)
        key_last = jnp.where(in_last, kf, 0.0).astype(jnp.bfloat16)
        grad_scores = (_dot(grad, value, 1, 1) * weight).astype(jnp.bfloat16)
        scores = (_dot(query, key, 1, 1) * weight).astype(jnp.bfloat16)
        dqs[at, :] = _dot(grad_scores, key, 1, 0) + _dot(grad_first, state_a, 1, 0)
        dks[at, :] = _dot(grad_scores, query, 0, 0) + _dot(value_last, state_b, 1, 1)
        dvs[at, :] = _dot(scores, grad, 0, 0) + _dot(key_last, state_b, 1, 0)
    for ref, scr in ((dq_ref, dqs), (dk_ref, dks), (dv_ref, dvs)):
        ref[...] = scr[...].reshape(n, heads, d).astype(ref.dtype)


def local_states(chunk, heads, place, lengths, arrays):
    n, total, d = arrays[0].shape
    slab = pl.BlockSpec((n, heads, d), lambda _: (0, chunk, 0))
    smem = pl.BlockSpec(memory_space=pltpu.SMEM)
    half = jax.ShapeDtypeStruct((2, heads // 2, d, d), jnp.bfloat16)
    whole = pl.BlockSpec((2, heads // 2, d, d), lambda _: (0, 0, 0, 0))
    return pl.pallas_call(
        states_kernel,
        grid=(1,),
        out_shape=(half, half),
        in_specs=[smem, smem] + [slab] * 4,
        out_specs=(whole, whole),
        scratch_shapes=[pltpu.VMEM((n * heads, d), jnp.float32)] * 4,
        compiler_params=pltpu.CompilerParams(vmem_limit_bytes=VMEM),
        cost_estimate=pl.CostEstimate(
            flops=4 * n * heads * d * d,
            bytes_accessed=8 * n * heads * d + 8 * heads * d * d,
            transcendentals=0,
        ),
        name="states",
    )(place, lengths, *arrays)


def local_grads(chunk, heads, scaling, place, lengths, arrays, mine, got, before):
    n, total, d = arrays[0].shape
    slab = pl.BlockSpec((n, heads, d), lambda _: (0, chunk, 0))
    smem = pl.BlockSpec(memory_space=pltpu.SMEM)
    whole = pl.BlockSpec((2, heads // 2, d, d), lambda _: (0, 0, 0, 0))
    out = jax.ShapeDtypeStruct((n, total, d), jnp.bfloat16)
    return pl.pallas_call(
        functools.partial(grads_kernel, scaling),
        grid=(1,),
        out_shape=(out, out, out),
        in_specs=[smem, smem]
        + [slab] * 4
        + [whole] * 2
        + [pl.BlockSpec(memory_space=pl.ANY)] * len(before),
        out_specs=(slab, slab, slab),
        scratch_shapes=[pltpu.VMEM((n * heads, d), jnp.float32)] * 7,
        input_output_aliases={8 + i: i for i in range(len(before))},
        compiler_params=pltpu.CompilerParams(vmem_limit_bytes=VMEM),
        cost_estimate=pl.CostEstimate(
            flops=2 * 8 * n * heads * d * d,
            bytes_accessed=14 * n * heads * d + 8 * heads * d * d,
            transcendentals=0,
        ),
        name="grads",
    )(place, lengths, *arrays, mine, got, *before)


def local(seq_size, head_size, queries, key_heads, value_heads, grad_output, doc_lengths):
    arrays = (queries, key_heads, value_heads, grad_output)
    n, heads, d = queries.shape
    tokens_all = n * seq_size * head_size
    scaling = 1.0 / math.sqrt(d * (tokens_all // 2))
    head_bits = _log2(head_size)
    low_bits = _log2(seq_size) // 2
    levels = head_bits + low_bits
    top = seq_size >> low_bits
    chunk_heads = max(heads // CHUNKS, min(heads, 1 << levels))
    chunks = heads // chunk_heads

    head_at, seq_at = lax.axis_index("head"), lax.axis_index("seq")
    device = (seq_at * head_size + head_at).astype(jnp.int32)
    bits = [(device >> level) & 1 for level in range(levels)]
    flip = sum(bit * (chunk_heads >> (level + 1)) for level, bit in enumerate(bits))
    place = jnp.stack([device, flip]).astype(jnp.int32)

    ends = jnp.cumsum(doc_lengths)

    def same(p, q):
        start = jnp.max(jnp.where(ends <= q, ends, 0))
        return (start <= p).astype(jnp.float32)

    def pair(a, b):
        return jnp.stack([a, b]).reshape(2, 1, 1, 1)

    up_coef, down_coef = [], []
    for level, bit in enumerate(bits):
        group = (device >> (level + 1)) << (level + 1)
        first_lo = group * n
        first_hi = (group + (1 << level)) * n
        last_lo = first_hi - 1
        last_hi = (group + (2 << level)) * n - 1
        is_hi = bit == 1
        lasts = same(last_lo, last_hi)
        firsts = same(first_lo, first_hi)
        join = same(last_lo, first_hi)
        one, zero = jnp.float32(1.0), jnp.float32(0.0)
        up_coef.append(
            (
                pair(jnp.where(is_hi, one, lasts), jnp.where(is_hi, firsts, one)),
                pair(jnp.where(is_hi, lasts, one), jnp.where(is_hi, one, firsts)),
            )
        )
        down_coef.append(
            (
                pair(jnp.where(is_hi, firsts, one), jnp.where(is_hi, one, lasts)),
                pair(jnp.where(is_hi, join, zero), jnp.where(is_hi, zero, join)),
                pair(jnp.where(is_hi, one, firsts), jnp.where(is_hi, lasts, one)),
                pair(jnp.where(is_hi, zero, join), jnp.where(is_hi, join, zero)),
            )
        )
    span = (1 << levels) * n
    group = device >> levels
    top_coef = []
    for step in range(1, top):
        top_coef.append(
            (
                same((group - step + 1) * span - 1, group * span),
                same((group + 1) * span - 1, (group + step) * span),
            )
        )

    def swap(x, level):
        if level < head_bits:
            bit = 1 << level
            return lax.ppermute(x, "head", [(i, i ^ bit) for i in range(head_size)])
        bit = 1 << (level - head_bits)
        return lax.ppermute(x, "seq", [(i, i ^ bit) for i in range(seq_size)])

    def shift(x, step):
        step = step << low_bits
        moves = [(i, i + step) for i in range(seq_size) if 0 <= i + step < seq_size]
        return lax.ppermute(x, "seq", moves)

    def f32(x):
        return x.astype(jnp.float32)

    def b16(x):
        return x.astype(jnp.bfloat16)

    def scan(keep, send):
        own, got = [], []
        for level in range(levels):
            own.append(keep)
            got.append(swap(send, level))
            c_own, c_got = up_coef[level]
            if level + 1 < levels:
                half = keep.shape[1] // 2
                o, g = own[-1], got[-1]
                send = b16(c_own * f32(o[:, half:]) + c_got * f32(g[:, half:]))
                keep = c_own * f32(o[:, :half]) + c_got * f32(g[:, :half])
            else:
                total = b16(c_own * f32(own[-1]) + c_got * f32(got[-1]))
        state_a = state_b = 0.0
        for step in range(1, top):
            w_a, w_b = top_coef[step - 1]
            state_a = state_a + w_a * f32(shift(total[0], step))
            state_b = state_b + w_b * f32(shift(total[1], -step))
        state = jnp.stack([state_a, state_b])
        for level in reversed(range(levels)):
            m_in, m_got, s_in, s_own = down_coef[level]
            factor = jnp.float32(scaling if level == 0 else 1.0)
            mine = factor * (m_in * state + m_got * f32(got[level]))
            theirs = b16(factor * (s_in * state + s_own * f32(own[level])))
            theirs = swap(theirs, level)
            if level == 0:
                return b16(mine), theirs
            state = jnp.concatenate([mine, f32(theirs)], axis=1)

    parts = [
        local_states(c, chunk_heads, place, doc_lengths, arrays) for c in range(chunks)
    ]
    scanned = [scan(*part) for part in parts]
    outs = ()
    for c in range(chunks):
        outs = local_grads(
            c, chunk_heads, scaling, place, doc_lengths, arrays, *scanned[c], outs
        )
    return tuple(outs)


def solution(mesh):
    placed = P(("seq", "head"), None, None)
    return jax.shard_map(
        functools.partial(local, mesh.shape["seq"], mesh.shape["head"]),
        mesh=mesh,
        in_specs=(placed, placed, placed, placed, P()),
        out_specs=(placed, placed, placed),
        check_vma=False,
    )
```

```python
import functools
import math

import jax
import jax.numpy as jnp
from jax import lax
from jax.experimental import pallas as pl
from jax.experimental.pallas import tpu as pltpu
from jax.sharding import PartitionSpec as P

CHUNKS = 4
VMEM = 56 * 1024 * 1024
F32 = jnp.float32
B16 = jnp.bfloat16


def _log2(n):
    k = n.bit_length() - 1
    assert 1 << k == n
    return k


def _same(len_ref, *pairs):
    total = jnp.int32(0)
    split = [jnp.bool_(False)] * len(pairs)
    for k in range(len_ref.shape[0]):
        total = total + len_ref[k]
        split = [s | ((total > p) & (total <= q)) for s, (p, q) in zip(split, pairs)]
    return [jnp.where(s, F32(0.0), F32(1.0)) for s in split]


def _edges(len_ref, first, last):
    start, stop, total = jnp.int32(0), jnp.int32(2**30), jnp.int32(0)
    for k in range(len_ref.shape[0]):
        total = total + len_ref[k]
        start = jnp.where(total <= last, jnp.maximum(start, total), start)
        stop = jnp.where(total > first, jnp.minimum(stop, total), stop)
    return start, stop


def _dot(a, b, ca, cb):
    return lax.dot_general(
        a, b, (((ca,), (cb,)), ((), ())), preferred_element_type=F32
    )


def _pick(rows, d, start, stop, first):
    row = lax.broadcasted_iota(jnp.int32, (rows, d), 0)
    token, odd = first + (row >> 1), row & 1
    last, lead = token >= start, token < stop
    return [
        jnp.where(ok & (odd == parity), F32(1.0), F32(0.0)).astype(B16)
        for ok in (last, lead)
        for parity in (0, 1)
    ]


def states_kernel(
    steps, place_ref, len_ref, q_ref, k_ref, v_ref, g_ref, *rest
):
    keep_ref, send_ref, pick = rest[-3:]
    n, width, _, d = q_ref.shape
    rows = 2 * n
    step = pl.program_id(0)
    first = place_ref[0] * n

    @pl.when(step == 0)
    def _():
        start, stop = _edges(len_ref, first, first + n - 1)
        for i, w in enumerate(_pick(rows, d, start, stop, first)):
            pick[i] = w

    def fill(out_ref):
        for p in range(width):
            query, key, value, grad = (
                ref[:, p].reshape(rows, d) for ref in (q_ref, k_ref, v_ref, g_ref)
            )
            keys = jnp.concatenate([key * pick[0], key * pick[1]], axis=1)
            grads = jnp.concatenate([grad * pick[2], grad * pick[3]], axis=1)
            out_ref[0, p] = _dot(value, keys, 0, 0).astype(out_ref.dtype)
            out_ref[1, p] = _dot(query, grads, 0, 0).astype(out_ref.dtype)

    @pl.when(step < steps // 2)
    def _():
        fill(keep_ref)

    @pl.when(step >= steps // 2)
    def _():
        fill(send_ref)


def grads_kernel(
    scaling,
    steps,
    place_ref,
    len_ref,
    q_ref,
    k_ref,
    v_ref,
    g_ref,
    mine_ref,
    got_ref,
    *rest,
):
    dq_ref, dk_ref, dv_ref, pick, down, across = rest[-6:]
    n, width, _, d = q_ref.shape
    rows = 2 * n
    step = pl.program_id(0)
    first = place_ref[0] * n

    @pl.when(step == 0)
    def _():
        start, stop = _edges(len_ref, first, first + n - 1)
        for i, w in enumerate(_pick(rows, d, start, stop, first)):
            pick[i] = w
        for ref, later, earlier in ((down, 0, 1), (across, 1, 0)):
            t = lax.broadcasted_iota(jnp.int32, (rows, rows), later)
            s = lax.broadcasted_iota(jnp.int32, (rows, rows), earlier)
            same_head = ((t ^ s) & 1) == 0
            t, s = first + (t >> 1), first + (s >> 1)
            begin = jnp.zeros((rows, rows), jnp.int32)
            total = jnp.int32(0)
            for k in range(len_ref.shape[0]):
                total = total + len_ref[k]
                begin = jnp.where(t >= total, total, begin)
            live = same_head & (s <= t) & (s >= begin)
            ref[...] = jnp.where(live, F32(scaling), F32(0.0)).astype(B16)

    def fill(state_ref):
        for p in range(width):
            query, key, value, grad = (
                ref[:, p].reshape(rows, d) for ref in (q_ref, k_ref, v_ref, g_ref)
            )
            state_a = state_ref[0, p]
            state_b = state_ref[1, p]
            last0, last1, lead0, lead1 = (pick[i] for i in range(4))
            ts = _dot(grad, value, 1, 1).astype(B16) * down[...]
            st = _dot(value, grad, 1, 1).astype(B16) * across[...]
            sc = _dot(key, query, 1, 1).astype(B16) * across[...]
            cat = jnp.concatenate
            dq = _dot(ts, key, 1, 0) + _dot(
                cat([grad * lead0, grad * lead1], axis=1),
                cat([state_a[:, :d], state_a[:, d:]], axis=0),
                1,
                0,
            )
            dk = _dot(st, query, 1, 0) + _dot(
                cat([value * last0, value * last1], axis=1), state_b, 1, 1
            )
            dv = _dot(sc, grad, 1, 0) + _dot(
                cat([key * last0, key * last1], axis=1),
                cat([state_b[:, :d], state_b[:, d:]], axis=0),
                1,
                0,
            )
            for ref, x in ((dq_ref, dq), (dk_ref, dk), (dv_ref, dv)):
                ref[:, p] = x.astype(B16).reshape(n, 2, d)

    @pl.when(step < steps // 2)
    def _():
        fill(mine_ref)

    @pl.when(step >= steps // 2)
    def _():
        fill(got_ref)


class Plan:
    def __init__(self, seq_size, head_size, n, heads, d, place, lengths):
        self.n, self.d, self.seq_size, self.head_size = n, d, seq_size, head_size
        self.head_bits, self.seq_bits = _log2(head_size), _log2(seq_size)
        self.scaling = 1.0 / math.sqrt(d * (n * seq_size * head_size // 2))
        pairs = heads // 2
        self.part = max(pairs // CHUNKS, min(pairs, head_size))
        self.chunks = pairs // self.part
        self.width = min(2, self.part >> self.head_bits)
        self.steps = self.part // self.width
        self.total = pairs
        self.place, self.lengths = place, lengths

    def token_spec(self, chunk):
        n, d, width, steps = self.n, self.d, self.width, self.steps
        return pl.BlockSpec(
            (n, width, 2, d),
            lambda i, place, _: (0, chunk * steps + (i ^ place[1]), 0, 0),
        )

    def half_specs(self):
        half = self.steps // 2
        shape = (2, self.width, self.d, 2 * self.d)
        low = pl.BlockSpec(shape, lambda i, *_: (0, jnp.minimum(i, half - 1), 0, 0))
        high = pl.BlockSpec(shape, lambda i, *_: (0, jnp.maximum(i - half, 0), 0, 0))
        return [low, high]

    def call(self, body, name, grid, ins, in_specs, outs, out_specs, scratch, cost, **kw):
        return pl.pallas_call(
            body,
            grid_spec=pltpu.PrefetchScalarGridSpec(
                num_scalar_prefetch=2,
                grid=grid,
                in_specs=in_specs,
                out_specs=out_specs,
                scratch_shapes=scratch,
            ),
            out_shape=outs,
            compiler_params=pltpu.CompilerParams(vmem_limit_bytes=VMEM),
            cost_estimate=pl.CostEstimate(
                flops=cost[0], bytes_accessed=cost[1], transcendentals=0
            ),
            name=name,
            **kw,
        )(self.place, self.lengths, *ins)

    def states(self, chunk, arrays, after):
        rows, d = 2 * self.n, self.d
        shape = (2, self.part // 2, d, 2 * d)
        return self.call(
            functools.partial(states_kernel, self.steps),
            "states",
            (self.steps,),
            [*arrays, *after],
            [self.token_spec(chunk)] * 4 + [pl.BlockSpec(memory_space=pl.ANY)] * len(after),
            (jax.ShapeDtypeStruct(shape, F32), jax.ShapeDtypeStruct(shape, B16)),
            self.half_specs(),
            [pltpu.VMEM((4, rows, d), B16)],
            (8 * rows * d * d * self.part, 8 * rows * d * self.part),
        )

    def grads(self, chunk, arrays, mine, got, before, after):
        rows, d = 2 * self.n, self.d
        token = self.token_spec(chunk)
        anywhere = pl.BlockSpec(memory_space=pl.ANY)
        out = jax.ShapeDtypeStruct((self.n, self.total, 2, d), B16)
        return self.call(
            functools.partial(grads_kernel, self.scaling, self.steps),
            "grads",
            (self.steps,),
            [*arrays, mine, got, *before, *after],
            [token] * 4 + self.half_specs() + [anywhere] * (len(before) + len(after)),
            (out, out, out),
            [token] * 3,
            [
                pltpu.VMEM((4, rows, d), B16),
                pltpu.VMEM((rows, rows), B16),
                pltpu.VMEM((rows, rows), B16),
            ],
            (20 * rows * d * d * self.part, 16 * rows * d * self.part),
            input_output_aliases={8 + i: i for i in range(len(before))},
        )

    def combine(self, name, body, ins, outs, after):
        specs = [
            pl.BlockSpec((1, *x.shape[1:]), (lambda i, *_: (i, 0, 0, 0)) if x.shape[0] == 2
                         else (lambda i, *_: (0, 0, 0, 0)))
            for x in (*ins, *outs)
        ]
        count = len(ins)
        moved = sum(math.prod(x.shape) * jnp.dtype(x.dtype).itemsize for x in (*ins, *outs))

        def kernel(place_ref, len_ref, *refs):
            device = place_ref[0]
            body(pl.program_id(0), device, len_ref, refs[:count], refs[-len(outs):])

        return self.call(
            kernel,
            name,
            (2,),
            [*ins, *after],
            specs[:count] + [pl.BlockSpec(memory_space=pl.ANY)] * len(after),
            tuple(outs),
            specs[count:],
            [],
            (moved, moved),
        )

    def level(self, device, len_ref, level):
        n = self.n
        group = (device >> (level + 1)) << (level + 1)
        middle = (group + (1 << level)) * n
        begin, end = group * n, (group + (2 << level)) * n
        lasts, firsts, join = _same(
            len_ref, (middle - 1, end - 1), (begin, middle), (middle - 1, middle)
        )
        return (device >> level) & 1 == 1, lasts, firsts, join

    def up_weights(self, which, device, len_ref, level):
        hi, lasts, firsts, _ = self.level(device, len_ref, level)
        one = F32(1.0)
        own = jnp.where(which == 0, jnp.where(hi, one, lasts), jnp.where(hi, firsts, one))
        got = jnp.where(which == 0, jnp.where(hi, lasts, one), jnp.where(hi, one, firsts))
        return own, got

    def down_weights(self, which, device, len_ref, level):
        hi, lasts, firsts, join = self.level(device, len_ref, level)
        one, zero = F32(1.0), F32(0.0)
        through = jnp.where(which == 0, firsts, lasts)
        mine_far = hi == (which == 0)
        m_in = jnp.where(mine_far, through, one)
        m_got = jnp.where(mine_far, join, zero)
        s_in = jnp.where(mine_far, one, through)
        s_own = jnp.where(mine_far, zero, join)
        return m_in, m_got, s_in, s_own

    def unit_weight(self, which, device, len_ref, level):
        n, bits = self.n, self.head_bits
        begin = ((device >> bits) << bits) * n
        end = begin + (n << bits)
        middle = (((device >> (level + 1)) << (level + 1)) + (1 << level)) * n
        hi = (device >> level) & 1 == 1
        ahead, behind = _same(len_ref, (middle - 1, begin), (end - 1, middle))
        return jnp.where(
            which == 0, jnp.where(hi, ahead, F32(0.0)), jnp.where(hi, F32(0.0), behind)
        )

    def swap(self, x, level):
        if level < self.head_bits:
            moves = [(i, i ^ (1 << level)) for i in range(self.head_size)]
            return lax.ppermute(x, "head", moves)
        bit = 1 << (level - self.head_bits)
        return lax.ppermute(x, "seq", [(i, i ^ bit) for i in range(self.seq_size)])

    def stages(self, chunk, arrays):
        d, bits, last = self.d, self.head_bits, self.head_bits + self.seq_bits - 1
        own, got, here = [], [], {}

        def shaped(pairs, dtype, lead=2):
            return jax.ShapeDtypeStruct((lead, pairs, d, 2 * d), dtype)

        def first(after):
            keep, send = self.states(chunk, arrays, after)
            own.append(keep)
            here["got"] = self.swap(send, 0)
            return keep

        def up(level, after):
            got.append(here["got"])
            pairs = own[-1].shape[1]
            if level + 1 < bits:
                half = pairs // 2

                def body(which, device, len_ref, ins, outs):
                    o, g = self.up_weights(which, device, len_ref, level)
                    x = o * ins[0][0] + g * ins[1][0].astype(F32)
                    outs[0][0] = x[:half]
                    outs[1][0] = x[half:].astype(B16)

                outs = [shaped(half, F32), shaped(half, B16)]
                keep, send = self.combine("up", body, [own[-1], got[-1]], outs, after)
                own.append(keep)
            else:

                def body(which, device, len_ref, ins, outs):
                    o, g = self.up_weights(which, device, len_ref, level)
                    x = o * ins[0][0] + g * ins[1][0].astype(F32)
                    outs[0][0] = x
                    outs[1][0] = x.astype(B16)

                outs = [shaped(pairs, F32), shaped(pairs, B16)]
                keep, send = self.combine("total", body, [own[-1], got[-1]], outs, after)
                here["total"] = keep
            here["got"] = self.swap(send, level + 1)
            return keep

        def across(level, after):
            ins = [here["total"], here["got"]]
            if "state" in here:
                ins.append(here["state"])
            pairs = ins[0].shape[1]
            final = level + 1 == last

            def body(which, device, len_ref, ins, outs):
                o, g = self.up_weights(which, device, len_ref, level)
                other = ins[1][0].astype(F32)
                x = o * ins[0][0] + g * other
                y = self.unit_weight(which, device, len_ref, level) * other
                if len(ins) > 2:
                    y = y + ins[2][0]
                outs[0][0] = y
                if final:

                    @pl.when(which == ((device >> last) & 1))
                    def _():
                        outs[1][0] = x.astype(B16)

                else:
                    outs[1][0] = x.astype(B16)
                    outs[2][0] = x

            outs = [shaped(pairs, F32), shaped(pairs, B16, 1 if final else 2)]
            if not final:
                outs.append(shaped(pairs, F32))
            state, send, *total = self.combine("across", body, ins, outs, after)
            here["state"] = state
            here["total"] = total[0] if total else None
            here["got"] = self.swap(send, level + 1)
            return state

        def down(level, after):
            top = level == bits - 1
            ins = [here["state"], here["got"], own[level], got[level]]
            pairs = own[level].shape[1]
            half = pairs // 2
            factor = self.scaling if level == 0 else 1.0

            def body(which, device, len_ref, ins, outs):
                m_in, m_got, s_in, s_own = self.down_weights(which, device, len_ref, level)
                m_in, m_got, s_in, s_own = (
                    factor * w for w in (m_in, m_got, s_in, s_own)
                )
                if top:
                    w = self.unit_weight(which, device, len_ref, last)
                    parts = [(slice(None), ins[0][0] + w * ins[1][0].astype(F32))]
                else:
                    parts = [
                        (slice(0, half), ins[0][0]),
                        (slice(half, pairs), ins[1][0].astype(F32)),
                    ]
                for at, x in parts:
                    own_x, got_x = ins[2][0, at], ins[3][0, at].astype(F32)
                    outs[0][0, at] = (m_in * x + m_got * got_x).astype(outs[0].dtype)
                    outs[1][0, at] = (s_in * x + s_own * own_x).astype(B16)

            outs = [shaped(pairs, B16 if level == 0 else F32), shaped(pairs, B16)]
            here["state"], send = self.combine("down", body, ins, outs, after)
            here["got"] = self.swap(send, level)
            return here["state"]

        def final(before, after):
            return self.grads(chunk, arrays, here["state"], here["got"], before, after)

        steps = [first]
        steps += [functools.partial(up, level) for level in range(bits)]
        steps += [functools.partial(across, level) for level in range(bits, last)]
        steps += [functools.partial(down, level) for level in reversed(range(bits))]
        return steps + [final]


def local(seq_size, head_size, queries, key_heads, value_heads, grad_output, doc_lengths):
    n, heads, d = queries.shape
    arrays = tuple(
        x.reshape(n, heads // 2, 2, d)
        for x in (queries, key_heads, value_heads, grad_output)
    )
    device = (lax.axis_index("seq") * head_size + lax.axis_index("head")).astype(jnp.int32)
    plan = Plan(seq_size, head_size, n, heads, d, None, doc_lengths)
    flip = sum(
        ((device >> level) & 1) * (plan.steps >> (level + 1))
        for level in range(plan.head_bits)
    )
    plan.place = jnp.stack([device, flip]).astype(jnp.int32)
    stages = [plan.stages(chunk, arrays) for chunk in range(plan.chunks)]
    count = len(stages[0])
    outs, after = (), ()
    for wave in range(count + plan.chunks - 1):
        for chunk in reversed(range(plan.chunks)):
            stage = wave - chunk
            if not 0 <= stage < count:
                continue
            if stage + 1 < count:
                after = (stages[chunk][stage](after),)
            else:
                outs = stages[chunk][stage](outs, after)
    return tuple(x.reshape(n, heads, d) for x in outs)


def solution(mesh):
    placed = P(("seq", "head"), None, None)
    return jax.shard_map(
        functools.partial(local, mesh.shape["seq"], mesh.shape["head"]),
        mesh=mesh,
        in_specs=(placed, placed, placed, placed, P()),
        out_specs=(placed, placed, placed),
        check_vma=False,
    )
```

```python
import functools
import math

import jax
import jax.numpy as jnp
from jax import lax
from jax.experimental import pallas as pl
from jax.experimental.pallas import tpu as pltpu
from jax.sharding import PartitionSpec as P

CHUNKS = 4
VMEM = 24 * 1024 * 1024
F32 = jnp.float32
B16 = jnp.bfloat16
IN_VMEM = pl.BlockSpec(memory_space=pltpu.VMEM)
IN_SMEM = pl.BlockSpec(memory_space=pltpu.SMEM)
IN_HBM = pl.BlockSpec(memory_space=pltpu.HBM)
ANYWHERE = pl.BlockSpec(memory_space=pl.ANY)


def _log2(n):
    k = n.bit_length() - 1
    assert 1 << k == n
    return k


def _same(len_ref, pairs):
    total = jnp.int32(0)
    split = [jnp.bool_(False)] * len(pairs)
    for k in range(len_ref.shape[0]):
        total = total + len_ref[k]
        split = [s | ((total > p) & (total <= q)) for s, (p, q) in zip(split, pairs)]
    return [jnp.where(s, F32(0.0), F32(1.0)) for s in split]


def _edges(len_ref, first, last):
    start, stop, total = jnp.int32(0), jnp.int32(2**30), jnp.int32(0)
    for k in range(len_ref.shape[0]):
        total = total + len_ref[k]
        start = jnp.where(total <= last, jnp.maximum(start, total), start)
        stop = jnp.where(total > first, jnp.minimum(stop, total), stop)
    return start, stop


def _dot(a, b, ca, cb):
    return lax.dot_general(
        a, b, (((ca,), (cb,)), ((), ())), preferred_element_type=F32
    )


def states_kernel(chunk, place_ref, len_ref, *refs):
    tokens, (keep_ref, send_ref, head_ref) = refs[:4], refs[-10:-7]
    slabs, wide, sems = refs[-7:-3], refs[-3:-1], refs[-1]
    n, _, d = tokens[0].shape
    heads = slabs[0].shape[1]
    half = heads // 2
    copies = [
        pltpu.make_async_copy(
            ref.at[:, pl.ds(chunk * heads, heads), :], slab, sems.at[i]
        )
        for i, (ref, slab) in enumerate(zip(tokens, slabs))
    ]
    for copy in copies:
        copy.start()
    first = place_ref[0] * n
    flip = place_ref[1]
    start, stop = _edges(len_ref, first, first + n - 1)
    row = lax.broadcasted_iota(jnp.int32, (n, d), 0) + first
    weights = (
        jnp.where(row < stop, F32(1.0), F32(0.0)).astype(B16),
        jnp.where(row >= start, F32(1.0), F32(0.0)).astype(B16),
    )
    for i, (copy, slab) in enumerate(zip(copies, slabs)):
        scr = wide[i % 2]
        copy.wait()
        scr[...] = slab[...].astype(F32).reshape(n * heads, d)
        for h in range(heads):
            head_ref[i, h] = scr[pl.ds(h, n, stride=heads), :].astype(B16)
    for r in range(heads):
        h = r ^ flip
        out, o = (keep_ref, r) if r < half else (send_ref, r - half)
        query, key, value, grad = (head_ref[i, h] for i in range(4))
        out[0, o] = _dot(key * weights[1], value, 0, 0).astype(out.dtype)
        out[1, o] = _dot(query, grad * weights[0], 0, 0).astype(out.dtype)


def grads_kernel(chunk, scaling, place_ref, len_ref, head_ref, mine_ref, got_ref, *refs):
    outs, token_ref = refs[-11:-8], refs[-8]
    wide, slabs, sems = refs[-7:-4], refs[-4:-1], refs[-1]
    token_ref[...] = jnp.zeros(token_ref.shape, token_ref.dtype)
    _, heads, n, d = head_ref.shape
    half = heads // 2
    first = place_ref[0] * n
    flip = place_ref[1]
    start, stop = _edges(len_ref, first, first + n - 1)
    row = lax.broadcasted_iota(jnp.int32, (n, d), 0) + first
    lead = jnp.where(row < stop, F32(1.0), F32(0.0))
    last = jnp.where(row >= start, F32(1.0), F32(0.0))
    last16 = last.astype(B16)

    def live(later):
        t = lax.broadcasted_iota(jnp.int32, (n, n), later) + first
        s = lax.broadcasted_iota(jnp.int32, (n, n), 1 - later) + first
        begin = jnp.zeros((n, n), jnp.int32)
        total = jnp.int32(0)
        for k in range(len_ref.shape[0]):
            total = total + len_ref[k]
            begin = jnp.where(t >= total, total, begin)
        return jnp.where((s <= t) & (s >= begin), F32(scaling), F32(0.0))

    down, across = live(0), live(1)
    cat = jnp.concatenate
    for r in range(heads):
        h = r ^ flip
        ref, o = (mine_ref, r) if r < half else (got_ref, r - half)
        state_a, state_b = ref[0, o], ref[1, o]
        query, key, value, grad = (head_ref[i, h] for i in range(4))
        x = _dot(grad, cat([value, state_a], axis=0), 1, 1)
        y = _dot(value, cat([grad, state_b], axis=0), 1, 1)
        z = _dot(key, query, 1, 1)
        ts = (x[:, :n] * down).astype(B16)
        st = (y[:, :n] * across).astype(B16)
        sc = (z * across).astype(B16)
        at = pl.ds(h, n, stride=heads)
        wide[0][at, :] = _dot(ts, key, 1, 0) + x[:, n:] * lead
        wide[1][at, :] = _dot(st, query, 1, 0) + y[:, n:] * last
        wide[2][at, :] = _dot(
            cat([sc, key * last16], axis=1), cat([grad, state_b], axis=0), 1, 0
        )
    copies = []
    for i, (scr, slab, out) in enumerate(zip(wide, slabs, outs)):
        slab[...] = scr[...].reshape(n, heads, d).astype(B16)
        copy = pltpu.make_async_copy(
            slab, out.at[:, pl.ds(chunk * heads, heads), :], sems.at[i]
        )
        copy.start()
        copies.append(copy)
    for copy in copies:
        copy.wait()


class Plan:
    def __init__(self, seq_size, head_size, n, heads, d, lengths):
        self.n, self.d, self.seq_size, self.head_size = n, d, seq_size, head_size
        self.head_bits, self.seq_bits = _log2(head_size), _log2(seq_size)
        self.levels = self.head_bits + self.seq_bits
        self.scaling = 1.0 / math.sqrt(d * (n * seq_size * head_size // 2))
        self.part = max(heads // CHUNKS, min(heads, head_size))
        self.chunks = heads // self.part
        self.total = heads
        self.lengths = lengths
        device = lax.axis_index("seq") * head_size + lax.axis_index("head")
        device = device.astype(jnp.int32)
        flip = sum(
            ((device >> level) & 1) * (self.part >> (level + 1))
            for level in range(self.head_bits)
        )
        self.place = jnp.stack([device, flip]).astype(jnp.int32)
        self.index = {}
        for level in range(self.levels):
            names = ["up_own", "up_got"]
            if level < self.head_bits:
                names += ["m_in", "m_got", "s_in", "s_own"]
            else:
                names += ["unit"]
            for name in names + (["pick"] if level + 1 == self.levels else []):
                self.index[name, level] = len(self.index)

    def call(self, body, name, ins, in_specs, outs, out_specs, scratch, cost, **kw):
        return pl.pallas_call(
            body,
            in_specs=in_specs,
            out_specs=out_specs,
            out_shape=outs,
            scratch_shapes=scratch,
            compiler_params=pltpu.CompilerParams(vmem_limit_bytes=VMEM),
            cost_estimate=pl.CostEstimate(
                flops=cost[0], bytes_accessed=cost[1], transcendentals=0
            ),
            name=name,
            **kw,
        )(*ins)

    def states(self, chunk, arrays, after):
        n, d, part = self.n, self.d, self.part
        shape = (2, part // 2, d, d)
        return self.call(
            functools.partial(states_kernel, chunk),
            "states",
            [self.place, self.lengths, *arrays, *after],
            [IN_SMEM] * 2 + [IN_HBM] * 4 + [ANYWHERE] * len(after),
            (
                jax.ShapeDtypeStruct(shape, F32),
                jax.ShapeDtypeStruct(shape, B16),
                jax.ShapeDtypeStruct((4, part, n, d), B16),
            ),
            [IN_VMEM] * 3,
            [pltpu.VMEM((n, part, d), B16)] * 4
            + [pltpu.VMEM((n * part, d), F32)] * 2
            + [pltpu.SemaphoreType.DMA((4,))],
            (4 * n * d * d * part, 16 * n * d * part),
        )

    def grads(self, chunk, heads, mine, got, before, after):
        n, d, part = self.n, self.d, self.part
        out = jax.ShapeDtypeStruct((n, self.total, d), B16)
        return self.call(
            functools.partial(grads_kernel, chunk, self.scaling),
            "grads",
            [self.place, self.lengths, heads, mine, got, *before, *after],
            [IN_SMEM] * 2
            + [IN_VMEM] * 3
            + [IN_HBM] * len(before)
            + [ANYWHERE] * len(after),
            (out, out, out, jax.ShapeDtypeStruct((8, 128), F32)),
            [IN_HBM] * 3 + [IN_VMEM],
            [pltpu.VMEM((n * part, d), F32)] * 3
            + [pltpu.VMEM((n, part, d), B16)] * 3
            + [pltpu.SemaphoreType.DMA((3,))],
            (16 * n * d * d * part, 16 * n * d * part),
            input_output_aliases={5 + i: i for i in range(len(before))},
        )

    def weights(self, after):
        n, bits = self.n, self.head_bits

        def kernel(place_ref, len_ref, *refs):
            out = refs[-1]
            device = place_ref[0]
            begin = ((device >> bits) << bits) * n
            end = begin + (n << bits)
            pairs = []
            for level in range(self.levels):
                group = (device >> (level + 1)) << (level + 1)
                low, high = group * n, (group + (2 << level)) * n
                middle = (group + (1 << level)) * n
                pairs += [(middle - 1, high - 1), (low, middle)]
                if level < bits:
                    pairs += [(middle - 1, middle)]
                else:
                    pairs += [(middle - 1, begin), (end - 1, middle)]
            same = _same(len_ref, pairs)
            one, zero = F32(1.0), F32(0.0)

            def put(name, level, a, b):
                out[2 * self.index[name, level]] = a
                out[2 * self.index[name, level] + 1] = b

            for level in range(self.levels):
                hi = (device >> level) & 1 == 1
                lasts, firsts = same[0], same[1]
                put("up_own", level, jnp.where(hi, one, lasts), jnp.where(hi, firsts, one))
                put("up_got", level, jnp.where(hi, lasts, one), jnp.where(hi, one, firsts))
                if level < bits:
                    join = same[2]
                    same = same[3:]
                    put("m_in", level, jnp.where(hi, firsts, one), jnp.where(hi, one, lasts))
                    put("m_got", level, jnp.where(hi, join, zero), jnp.where(hi, zero, join))
                    put("s_in", level, jnp.where(hi, one, firsts), jnp.where(hi, lasts, one))
                    put("s_own", level, jnp.where(hi, zero, join), jnp.where(hi, join, zero))
                else:
                    ahead, behind = same[2], same[3]
                    same = same[4:]
                    put("unit", level, jnp.where(hi, ahead, zero), jnp.where(hi, zero, behind))
                if level + 1 == self.levels:
                    put("pick", level, jnp.where(hi, zero, one), jnp.where(hi, one, zero))

        self.scalars = self.call(
            kernel,
            "weights",
            [self.place, self.lengths, *after],
            [IN_SMEM] * 2 + [ANYWHERE] * len(after),
            jax.ShapeDtypeStruct((2 * len(self.index),), F32),
            IN_SMEM,
            [],
            (1000, 1000),
        )

    def combine(self, name, body, ins, outs, after):
        moved = sum(math.prod(x.shape) * jnp.dtype(x.dtype).itemsize for x in (*ins, *outs))

        def kernel(scalar_ref, *refs):
            body(
                lambda name, level, which: scalar_ref[2 * self.index[name, level] + which],
                refs[: len(ins)],
                refs[len(refs) - len(outs) :],
            )

        return self.call(
            kernel,
            name,
            [self.scalars, *ins, *after],
            [IN_SMEM] + [IN_VMEM] * len(ins) + [ANYWHERE] * len(after),
            tuple(outs),
            [IN_VMEM] * len(outs),
            [],
            (moved, moved),
        )

    def swap(self, x, level):
        if level < self.head_bits:
            moves = [(i, i ^ (1 << level)) for i in range(self.head_size)]
            return lax.ppermute(x, "head", moves)
        bit = 1 << (level - self.head_bits)
        return lax.ppermute(x, "seq", [(i, i ^ bit) for i in range(self.seq_size)])

    def stages(self, chunk, arrays):
        d, bits, last = self.d, self.head_bits, self.levels - 1
        own, got, here = [], [], {}

        def shaped(heads, dtype, lead=2):
            return jax.ShapeDtypeStruct((lead, heads, d, d), dtype)

        def first(after):
            keep, send, here["heads"] = self.states(chunk, arrays, after)
            own.append(keep)
            here["got"] = self.swap(send, 0)
            if chunk == 0:
                self.weights((keep,))
            return keep

        def up(level, after):
            got.append(here["got"])
            heads = own[-1].shape[1]
            half = heads // 2 if level + 1 < bits else heads

            def body(w, ins, outs):
                for which in range(2):
                    o, g = w("up_own", level, which), w("up_got", level, which)
                    for h in range(heads):
                        x = o * ins[0][which, h] + g * ins[1][which, h].astype(F32)
                        if h < half:
                            outs[0][which, h] = x
                        if half == heads:
                            outs[1][which, h] = x.astype(B16)
                        elif h >= half:
                            outs[1][which, h - half] = x.astype(B16)

            outs = [shaped(half, F32), shaped(half, B16)]
            keep, send = self.combine("up", body, [own[-1], got[-1]], outs, after)
            if half < heads:
                own.append(keep)
            else:
                here["total"] = keep
            here["got"] = self.swap(send, level + 1)
            return keep

        def across(level, after):
            ins = [here["total"], here["got"]]
            if "state" in here:
                ins.append(here["state"])
            heads = ins[0].shape[1]
            final = level + 1 == last

            def body(w, ins, outs):
                for h in range(heads):
                    totals = []
                    for which in range(2):
                        other = ins[1][which, h].astype(F32)
                        x = w("up_own", level, which) * ins[0][which, h]
                        x = x + w("up_got", level, which) * other
                        y = w("unit", level, which) * other
                        if len(ins) > 2:
                            y = y + ins[2][which, h]
                        outs[0][which, h] = y
                        totals.append(x)
                        if not final:
                            outs[1][which, h] = x.astype(B16)
                            outs[2][which, h] = x
                    if final:
                        x = w("pick", last, 0) * totals[0] + w("pick", last, 1) * totals[1]
                        outs[1][0, h] = x.astype(B16)

            outs = [shaped(heads, F32), shaped(heads, B16, 1 if final else 2)]
            if not final:
                outs.append(shaped(heads, F32))
            state, send, *total = self.combine("across", body, ins, outs, after)
            here["state"] = state
            here["total"] = total[0] if total else None
            here["got"] = self.swap(send, level + 1)
            return state

        def down(level, after):
            top = level == bits - 1
            ins = [here["state"], here["got"], own[level], got[level]]
            heads = own[level].shape[1]
            half = heads // 2
            factor = self.scaling if level == 0 else 1.0

            def body(w, ins, outs):
                for which in range(2):
                    m_in, m_got, s_in, s_own = (
                        factor * w(name, level, which)
                        for name in ("m_in", "m_got", "s_in", "s_own")
                    )
                    for h in range(heads):
                        if top:
                            x = w("unit", last, which) * ins[1][0, h].astype(F32)
                            x = x + ins[0][which, h]
                        elif h < half:
                            x = ins[0][which, h]
                        else:
                            x = ins[1][which, h - half].astype(F32)
                        mine = m_in * x + m_got * ins[3][which, h].astype(F32)
                        theirs = s_in * x + s_own * ins[2][which, h]
                        outs[0][which, h] = mine.astype(outs[0].dtype)
                        outs[1][which, h] = theirs.astype(B16)

            outs = [shaped(heads, B16 if level == 0 else F32), shaped(heads, B16)]
            here["state"], send = self.combine("down", body, ins, outs, after)
            here["got"] = self.swap(send, level)
            return here["state"]

        def final(before, after):
            *outs, token = self.grads(
                chunk, here["heads"], here["state"], here["got"], before, after
            )
            return outs, token

        steps = [first]
        steps += [functools.partial(up, level) for level in range(bits)]
        steps += [functools.partial(across, level) for level in range(bits, last)]
        steps += [functools.partial(down, level) for level in reversed(range(bits))]
        return steps + [final]


def local(seq_size, head_size, queries, key_heads, value_heads, grad_output, doc_lengths):
    n, heads, d = queries.shape
    arrays = (queries, key_heads, value_heads, grad_output)
    plan = Plan(seq_size, head_size, n, heads, d, doc_lengths)
    stages = [plan.stages(chunk, arrays) for chunk in range(plan.chunks)]
    count = len(stages[0])
    outs, after = (), ()
    for wave in range(count + plan.chunks - 1):
        for chunk in reversed(range(plan.chunks)):
            stage = wave - chunk
            if not 0 <= stage < count:
                continue
            if stage + 1 < count:
                after = (stages[chunk][stage](after),)
            else:
                outs, token = stages[chunk][stage](outs, after)
                after = (token,)
    return tuple(outs)


def solution(mesh):
    placed = P(("seq", "head"), None, None)
    return jax.shard_map(
        functools.partial(local, mesh.shape["seq"], mesh.shape["head"]),
        mesh=mesh,
        in_specs=(placed, placed, placed, placed, P()),
        out_specs=(placed, placed, placed),
        check_vma=False,
    )
```

```python
import functools
import math

import jax
import jax.numpy as jnp
from jax import lax
from jax.experimental import pallas as pl
from jax.experimental.pallas import tpu as pltpu
from jax.sharding import PartitionSpec as P

CHUNKS = 4
VMEM = 24 * 1024 * 1024
VMEM_STATES = 59 * 1024 * 1024
VMEM_CHUNK = 18 * 1024 * 1024
F32 = jnp.float32
B16 = jnp.bfloat16
IN_VMEM = pl.BlockSpec(memory_space=pltpu.VMEM)
IN_SMEM = pl.BlockSpec(memory_space=pltpu.SMEM)
IN_HBM = pl.BlockSpec(memory_space=pltpu.HBM)
ANYWHERE = pl.BlockSpec(memory_space=pl.ANY)


def _log2(n):
    k = n.bit_length() - 1
    assert 1 << k == n
    return k


def _same(len_ref, pairs):
    total = jnp.int32(0)
    split = [jnp.bool_(False)] * len(pairs)
    for k in range(len_ref.shape[0]):
        total = total + len_ref[k]
        split = [s | ((total > p) & (total <= q)) for s, (p, q) in zip(split, pairs)]
    return [jnp.where(s, F32(0.0), F32(1.0)) for s in split]


def _edges(len_ref, first, last):
    start, stop, total = jnp.int32(0), jnp.int32(2**30), jnp.int32(0)
    for k in range(len_ref.shape[0]):
        total = total + len_ref[k]
        start = jnp.where(total <= last, jnp.maximum(start, total), start)
        stop = jnp.where(total > first, jnp.minimum(stop, total), stop)
    return start, stop


def _dot(a, b, ca, cb):
    return lax.dot_general(
        a, b, (((ca,), (cb,)), ((), ())), preferred_element_type=F32
    )


def states_kernel(chunk, place_ref, len_ref, *refs):
    tokens, (keep_ref, send_ref, head_ref) = refs[:4], refs[-10:-7]
    slabs, wide, sems = refs[-7:-3], refs[-3:-1], refs[-1]
    n, _, d = tokens[0].shape
    heads = slabs[0].shape[1]
    half = heads // 2
    copies = [
        pltpu.make_async_copy(
            ref.at[:, pl.ds(chunk * heads, heads), :], slab, sems.at[i]
        )
        for i, (ref, slab) in enumerate(zip(tokens, slabs))
    ]
    for copy in copies:
        copy.start()
    first = place_ref[0] * n
    flip = place_ref[1]
    start, stop = _edges(len_ref, first, first + n - 1)
    row = lax.broadcasted_iota(jnp.int32, (n, d), 0) + first
    weights = (
        jnp.where(row < stop, F32(1.0), F32(0.0)).astype(B16),
        jnp.where(row >= start, F32(1.0), F32(0.0)).astype(B16),
    )
    for i, (copy, slab) in enumerate(zip(copies, slabs)):
        scr = wide[i % 2]
        copy.wait()
        scr[...] = slab[...].astype(F32).reshape(n * heads, d)
        for h in range(heads):
            head_ref[i, h] = scr[pl.ds(h, n, stride=heads), :].astype(B16)
    for r in range(heads):
        h = r ^ flip
        out, o = (keep_ref, r) if r < half else (send_ref, r - half)
        query, key, value, grad = (head_ref[i, h] for i in range(4))
        out[0, o] = _dot(key * weights[1], value, 0, 0).astype(out.dtype)
        out[1, o] = _dot(query, grad * weights[0], 0, 0).astype(out.dtype)


def grads_kernel(chunk, scaling, place_ref, len_ref, head_ref, mine_ref, got_ref, *refs):
    outs, token_ref = refs[-11:-8], refs[-8]
    wide, slabs, sems = refs[-7:-4], refs[-4:-1], refs[-1]
    token_ref[...] = jnp.zeros(token_ref.shape, token_ref.dtype)
    _, heads, n, d = head_ref.shape
    half = heads // 2
    first = place_ref[0] * n
    flip = place_ref[1]
    start, stop = _edges(len_ref, first, first + n - 1)
    row = lax.broadcasted_iota(jnp.int32, (n, d), 0) + first
    lead = jnp.where(row < stop, F32(1.0), F32(0.0))
    last = jnp.where(row >= start, F32(1.0), F32(0.0))
    last16 = last.astype(B16)

    def live(later):
        t = lax.broadcasted_iota(jnp.int32, (n, n), later) + first
        s = lax.broadcasted_iota(jnp.int32, (n, n), 1 - later) + first
        begin = jnp.zeros((n, n), jnp.int32)
        total = jnp.int32(0)
        for k in range(len_ref.shape[0]):
            total = total + len_ref[k]
            begin = jnp.where(t >= total, total, begin)
        return jnp.where((s <= t) & (s >= begin), F32(scaling), F32(0.0))

    down, across = live(0), live(1)
    cat = jnp.concatenate
    for r in range(heads):
        h = r ^ flip
        ref, o = (mine_ref, r) if r < half else (got_ref, r - half)
        state_a, state_b = ref[0, o], ref[1, o]
        query, key, value, grad = (head_ref[i, h] for i in range(4))
        x = _dot(grad, cat([value, state_a], axis=0), 1, 1)
        y = _dot(value, cat([grad, state_b], axis=0), 1, 1)
        z = _dot(key, query, 1, 1)
        ts = (x[:, :n] * down).astype(B16)
        st = (y[:, :n] * across).astype(B16)
        sc = (z * across).astype(B16)
        at = pl.ds(h, n, stride=heads)
        wide[0][at, :] = _dot(ts, key, 1, 0) + x[:, n:] * lead
        wide[1][at, :] = _dot(st, query, 1, 0) + y[:, n:] * last
        wide[2][at, :] = _dot(
            cat([sc, key * last16], axis=1), cat([grad, state_b], axis=0), 1, 0
        )
    copies = []
    for i, (scr, slab, out) in enumerate(zip(wide, slabs, outs)):
        slab[...] = scr[...].reshape(n, heads, d).astype(B16)
        copy = pltpu.make_async_copy(
            slab, out.at[:, pl.ds(chunk * heads, heads), :], sems.at[i]
        )
        copy.start()
        copies.append(copy)
    for copy in copies:
        copy.wait()


class Plan:
    def __init__(self, seq_size, head_size, n, heads, d, lengths):
        self.n, self.d, self.seq_size, self.head_size = n, d, seq_size, head_size
        self.head_bits, self.seq_bits = _log2(head_size), _log2(seq_size)
        self.levels = self.head_bits + self.seq_bits
        self.scaling = 1.0 / math.sqrt(d * (n * seq_size * head_size // 2))
        self.part = max(heads // CHUNKS, min(heads, head_size))
        self.chunks = heads // self.part
        self.total = heads
        self.lengths = lengths
        device = lax.axis_index("seq") * head_size + lax.axis_index("head")
        device = device.astype(jnp.int32)
        flip = sum(
            ((device >> level) & 1) * (self.part >> (level + 1))
            for level in range(self.head_bits)
        )
        self.place = jnp.stack([device, flip]).astype(jnp.int32)
        self.index = {}
        for level in range(self.levels):
            names = ["up_own", "up_got"]
            if level < self.head_bits:
                names += ["m_in", "m_got", "s_in", "s_own"]
            else:
                names += ["unit"]
            for name in names + (["pick"] if level + 1 == self.levels else []):
                self.index[name, level] = len(self.index)

    def call(self, body, name, ins, in_specs, outs, out_specs, scratch, vmem=VMEM, **kw):
        return pl.pallas_call(
            body,
            in_specs=in_specs,
            out_specs=out_specs,
            out_shape=outs,
            scratch_shapes=scratch,
            compiler_params=pltpu.CompilerParams(vmem_limit_bytes=vmem),
            cost_estimate=pl.CostEstimate(flops=1, bytes_accessed=1, transcendentals=0),
            name=name,
            **kw,
        )(*ins)

    def states(self, chunk, arrays, after):
        n, d, part = self.n, self.d, self.part
        shape = (2, part // 2, d, d)
        return self.call(
            functools.partial(states_kernel, chunk),
            "states",
            [self.place, self.lengths, *arrays, *after],
            [IN_SMEM] * 2 + [IN_HBM] * 4 + [ANYWHERE] * len(after),
            (
                jax.ShapeDtypeStruct(shape, F32),
                jax.ShapeDtypeStruct(shape, B16),
                jax.ShapeDtypeStruct((4, part, n, d), B16),
            ),
            [IN_VMEM] * 3,
            [pltpu.VMEM((n, part, d), B16)] * 4
            + [pltpu.VMEM((n * part, d), F32)] * 2
            + [pltpu.SemaphoreType.DMA((4,))],
            VMEM_STATES - chunk * (VMEM_CHUNK // self.chunks),
        )

    def grads(self, chunk, heads, mine, got, before, after):
        n, d, part = self.n, self.d, self.part
        out = jax.ShapeDtypeStruct((n, self.total, d), B16)
        return self.call(
            functools.partial(grads_kernel, chunk, self.scaling),
            "grads",
            [self.place, self.lengths, heads, mine, got, *before, *after],
            [IN_SMEM] * 2
            + [IN_VMEM] * 3
            + [IN_HBM] * len(before)
            + [ANYWHERE] * len(after),
            (out, out, out, jax.ShapeDtypeStruct((8, 128), F32)),
            [IN_HBM] * 3 + [IN_VMEM],
            [pltpu.VMEM((n * part, d), F32)] * 3
            + [pltpu.VMEM((n, part, d), B16)] * 3
            + [pltpu.SemaphoreType.DMA((3,))],
            input_output_aliases={5 + i: i for i in range(len(before))},
        )

    def weights(self, after):
        n, bits = self.n, self.head_bits

        def kernel(place_ref, len_ref, *refs):
            out = refs[-1]
            device = place_ref[0]
            begin = ((device >> bits) << bits) * n
            end = begin + (n << bits)
            pairs = []
            for level in range(self.levels):
                group = (device >> (level + 1)) << (level + 1)
                low, high = group * n, (group + (2 << level)) * n
                middle = (group + (1 << level)) * n
                pairs += [(middle - 1, high - 1), (low, middle)]
                if level < bits:
                    pairs += [(middle - 1, middle)]
                else:
                    pairs += [(middle - 1, begin), (end - 1, middle)]
            same = _same(len_ref, pairs)
            one, zero = F32(1.0), F32(0.0)

            def put(name, level, a, b):
                out[2 * self.index[name, level]] = a
                out[2 * self.index[name, level] + 1] = b

            for level in range(self.levels):
                hi = (device >> level) & 1 == 1
                lasts, firsts = same[0], same[1]
                put("up_own", level, jnp.where(hi, one, lasts), jnp.where(hi, firsts, one))
                put("up_got", level, jnp.where(hi, lasts, one), jnp.where(hi, one, firsts))
                if level < bits:
                    join = same[2]
                    same = same[3:]
                    put("m_in", level, jnp.where(hi, firsts, one), jnp.where(hi, one, lasts))
                    put("m_got", level, jnp.where(hi, join, zero), jnp.where(hi, zero, join))
                    put("s_in", level, jnp.where(hi, one, firsts), jnp.where(hi, lasts, one))
                    put("s_own", level, jnp.where(hi, zero, join), jnp.where(hi, join, zero))
                else:
                    ahead, behind = same[2], same[3]
                    same = same[4:]
                    put("unit", level, jnp.where(hi, ahead, zero), jnp.where(hi, zero, behind))
                if level + 1 == self.levels:
                    put("pick", level, jnp.where(hi, zero, one), jnp.where(hi, one, zero))

        self.scalars = self.call(
            kernel,
            "weights",
            [self.place, self.lengths, *after],
            [IN_SMEM] * 2 + [ANYWHERE] * len(after),
            jax.ShapeDtypeStruct((2 * len(self.index),), F32),
            IN_SMEM,
            [],
        )

    def combine(self, name, body, ins, outs, after):
        def kernel(scalar_ref, *refs):
            body(
                lambda name, level, which: scalar_ref[2 * self.index[name, level] + which],
                refs[: len(ins)],
                refs[len(refs) - len(outs) :],
            )

        return self.call(
            kernel,
            name,
            [self.scalars, *ins, *after],
            [IN_SMEM] + [IN_VMEM] * len(ins) + [ANYWHERE] * len(after),
            tuple(outs),
            [IN_VMEM] * len(outs),
            [],
        )

    def swap(self, x, level):
        if level < self.head_bits:
            moves = [(i, i ^ (1 << level)) for i in range(self.head_size)]
            return lax.ppermute(x, "head", moves)
        bit = 1 << (level - self.head_bits)
        return lax.ppermute(x, "seq", [(i, i ^ bit) for i in range(self.seq_size)])

    def stages(self, chunk, arrays):
        d, bits, last = self.d, self.head_bits, self.levels - 1
        own, got, here = [], [], {}

        def shaped(heads, dtype, lead=2):
            return jax.ShapeDtypeStruct((lead, heads, d, d), dtype)

        def first(after):
            keep, send, here["heads"] = self.states(chunk, arrays, after)
            own.append(keep)
            here["got"] = self.swap(send, 0)
            if chunk == 0:
                self.weights((keep,))
            return keep

        def up(level, after):
            got.append(here["got"])
            heads = own[-1].shape[1]
            half = heads // 2 if level + 1 < bits else heads

            def body(w, ins, outs):
                for which in range(2):
                    o, g = w("up_own", level, which), w("up_got", level, which)
                    for h in range(heads):
                        x = o * ins[0][which, h] + g * ins[1][which, h].astype(F32)
                        if h < half:
                            outs[0][which, h] = x
                        if half == heads:
                            outs[1][which, h] = x.astype(B16)
                        elif h >= half:
                            outs[1][which, h - half] = x.astype(B16)

            outs = [shaped(half, F32), shaped(half, B16)]
            keep, send = self.combine("up", body, [own[-1], got[-1]], outs, after)
            if half < heads:
                own.append(keep)
            else:
                here["total"] = keep
            here["got"] = self.swap(send, level + 1)
            return keep

        def across(level, after):
            ins = [here["total"], here["got"]]
            if "state" in here:
                ins.append(here["state"])
            heads = ins[0].shape[1]
            final = level + 1 == last

            def body(w, ins, outs):
                for h in range(heads):
                    totals = []
                    for which in range(2):
                        other = ins[1][which, h].astype(F32)
                        x = w("up_own", level, which) * ins[0][which, h]
                        x = x + w("up_got", level, which) * other
                        y = w("unit", level, which) * other
                        if len(ins) > 2:
                            y = y + ins[2][which, h]
                        outs[0][which, h] = y
                        totals.append(x)
                        if not final:
                            outs[1][which, h] = x.astype(B16)
                            outs[2][which, h] = x
                    if final:
                        x = w("pick", last, 0) * totals[0] + w("pick", last, 1) * totals[1]
                        outs[1][0, h] = x.astype(B16)

            outs = [shaped(heads, F32), shaped(heads, B16, 1 if final else 2)]
            if not final:
                outs.append(shaped(heads, F32))
            state, send, *total = self.combine("across", body, ins, outs, after)
            here["state"] = state
            here["total"] = total[0] if total else None
            here["got"] = self.swap(send, level + 1)
            return state

        def down(level, after):
            top = level == bits - 1
            ins = [here["state"], here["got"], own[level], got[level]]
            heads = own[level].shape[1]
            half = heads // 2
            factor = self.scaling if level == 0 else 1.0

            def body(w, ins, outs):
                for which in range(2):
                    m_in, m_got, s_in, s_own = (
                        factor * w(name, level, which)
                        for name in ("m_in", "m_got", "s_in", "s_own")
                    )
                    for h in range(heads):
                        if top:
                            x = w("unit", last, which) * ins[1][0, h].astype(F32)
                            x = x + ins[0][which, h]
                        elif h < half:
                            x = ins[0][which, h]
                        else:
                            x = ins[1][which, h - half].astype(F32)
                        mine = m_in * x + m_got * ins[3][which, h].astype(F32)
                        theirs = s_in * x + s_own * ins[2][which, h]
                        outs[0][which, h] = mine.astype(outs[0].dtype)
                        outs[1][which, h] = theirs.astype(B16)

            outs = [shaped(heads, B16 if level == 0 else F32), shaped(heads, B16)]
            here["state"], send = self.combine("down", body, ins, outs, after)
            here["got"] = self.swap(send, level)
            return here["state"]

        def final(before, after):
            *outs, token = self.grads(
                chunk, here["heads"], here["state"], here["got"], before, after
            )
            return outs, token

        steps = [first]
        steps += [functools.partial(up, level) for level in range(bits)]
        steps += [functools.partial(across, level) for level in range(bits, last)]
        steps += [functools.partial(down, level) for level in reversed(range(bits))]
        return steps + [final]


def local(seq_size, head_size, queries, key_heads, value_heads, grad_output, doc_lengths):
    n, heads, d = queries.shape
    arrays = (queries, key_heads, value_heads, grad_output)
    plan = Plan(seq_size, head_size, n, heads, d, doc_lengths)
    stages = [plan.stages(chunk, arrays) for chunk in range(plan.chunks)]
    count = len(stages[0])
    outs, after = (), ()
    order = [(0, chunk) for chunk in range(plan.chunks)]
    for wave in range(1, count + plan.chunks - 1):
        for chunk in reversed(range(plan.chunks)):
            if 1 <= wave - chunk < count:
                order.append((wave - chunk, chunk))
    for stage, chunk in order:
        if stage + 1 < count:
            after = (stages[chunk][stage](after),)
        else:
            outs, token = stages[chunk][stage](outs, after)
            after = (token,)
    return tuple(outs)


def solution(mesh):
    placed = P(("seq", "head"), None, None)
    return jax.shard_map(
        functools.partial(local, mesh.shape["seq"], mesh.shape["head"]),
        mesh=mesh,
        in_specs=(placed, placed, placed, placed, P()),
        out_specs=(placed, placed, placed),
        check_vma=False,
    )
```

```python
import functools
import math

import jax
import jax.numpy as jnp
from jax import lax
from jax.experimental import pallas as pl
from jax.experimental.pallas import tpu as pltpu
from jax.sharding import PartitionSpec as P

CHUNKS = 4
VMEM = 24 * 1024 * 1024
VMEM_FIRST = 56 * 1024 * 1024
VMEM_NEXT = 46 * 1024 * 1024
F32 = jnp.float32
B16 = jnp.bfloat16
IN_VMEM = pl.BlockSpec(memory_space=pltpu.VMEM)
IN_SMEM = pl.BlockSpec(memory_space=pltpu.SMEM)
IN_HBM = pl.BlockSpec(memory_space=pltpu.HBM)
ANYWHERE = pl.BlockSpec(memory_space=pl.ANY)


def _log2(n):
    k = n.bit_length() - 1
    assert 1 << k == n
    return k


def _same(len_ref, pairs):
    total = jnp.int32(0)
    split = [jnp.bool_(False)] * len(pairs)
    for k in range(len_ref.shape[0]):
        total = total + len_ref[k]
        split = [s | ((total > p) & (total <= q)) for s, (p, q) in zip(split, pairs)]
    return [jnp.where(s, F32(0.0), F32(1.0)) for s in split]


def _edges(len_ref, first, last):
    start, stop, total = jnp.int32(0), jnp.int32(2**30), jnp.int32(0)
    for k in range(len_ref.shape[0]):
        total = total + len_ref[k]
        start = jnp.where(total <= last, jnp.maximum(start, total), start)
        stop = jnp.where(total > first, jnp.minimum(stop, total), stop)
    return start, stop


def _dot(a, b, ca, cb):
    return lax.dot_general(
        a, b, (((ca,), (cb,)), ((), ())), preferred_element_type=F32
    )


def states_kernel(chunks, weights, place_ref, len_ref, *refs):
    count = len(chunks)
    tokens, refs = refs[:4], refs[len(refs) - 2 * count - (weights is not None) - 5 :]
    if weights is not None:
        weights(place_ref, len_ref, refs[0])
        refs = refs[1:]
    keeps, head_refs, send_ref = refs[:count], refs[count : 2 * count], refs[2 * count]
    slab, wide, sems = refs[2 * count + 1], refs[-3:-1], refs[-1]
    n, _, d = tokens[0].shape
    heads = slab.shape[3]
    half = heads // 2
    copies = [
        [
            pltpu.make_async_copy(
                ref.at[:, pl.ds(chunk * heads, heads), :], slab.at[j, i], sems.at[j, i]
            )
            for i, ref in enumerate(tokens)
        ]
        for j, chunk in enumerate(chunks)
    ]
    for some in copies:
        for copy in some:
            copy.start()
    first = place_ref[0] * n
    flip = place_ref[1]
    start, stop = _edges(len_ref, first, first + n - 1)
    row = lax.broadcasted_iota(jnp.int32, (n, d), 0) + first
    lead = jnp.where(row < stop, F32(1.0), F32(0.0)).astype(B16)
    last = jnp.where(row >= start, F32(1.0), F32(0.0)).astype(B16)
    for j in range(count):
        for i in range(4):
            scr = wide[i % 2]
            copies[j][i].wait()
            scr[...] = slab[j, i].astype(F32).reshape(n * heads, d)
            for h in range(heads):
                head_refs[j][i, h] = scr[pl.ds(h, n, stride=heads), :].astype(B16)
        for r in range(heads):
            h = r ^ flip
            query, key, value, grad = (head_refs[j][i, h] for i in range(4))
            state_a = _dot(key * last, value, 0, 0)
            state_b = _dot(query, grad * lead, 0, 0)
            if r < half:
                keeps[j][0, r] = state_a
                keeps[j][1, r] = state_b
            else:
                send_ref[j, 0, r - half] = state_a.astype(B16)
                send_ref[j, 1, r - half] = state_b.astype(B16)


def grads_kernel(chunk, scaling, place_ref, len_ref, head_ref, mine_ref, got_ref, *refs):
    outs, token_ref = refs[-11:-8], refs[-8]
    wide, slabs, sems = refs[-7:-4], refs[-4:-1], refs[-1]
    token_ref[...] = jnp.zeros(token_ref.shape, token_ref.dtype)
    _, heads, n, d = head_ref.shape
    half = heads // 2
    first = place_ref[0] * n
    flip = place_ref[1]
    start, stop = _edges(len_ref, first, first + n - 1)
    row = lax.broadcasted_iota(jnp.int32, (n, d), 0) + first
    lead = jnp.where(row < stop, F32(1.0), F32(0.0))
    last = jnp.where(row >= start, F32(1.0), F32(0.0))
    last16 = last.astype(B16)

    def live(later):
        t = lax.broadcasted_iota(jnp.int32, (n, n), later) + first
        s = lax.broadcasted_iota(jnp.int32, (n, n), 1 - later) + first
        begin = jnp.zeros((n, n), jnp.int32)
        total = jnp.int32(0)
        for k in range(len_ref.shape[0]):
            total = total + len_ref[k]
            begin = jnp.where(t >= total, total, begin)
        return jnp.where((s <= t) & (s >= begin), F32(scaling), F32(0.0))

    down, across = live(0), live(1)
    cat = jnp.concatenate
    for r in range(heads):
        h = r ^ flip
        ref, o = (mine_ref, r) if r < half else (got_ref, r - half)
        state_a, state_b = ref[0, o], ref[1, o]
        query, key, value, grad = (head_ref[i, h] for i in range(4))
        x = _dot(grad, cat([value, state_a], axis=0), 1, 1)
        y = _dot(value, cat([grad, state_b], axis=0), 1, 1)
        z = _dot(key, query, 1, 1)
        ts = (x[:, :n] * down).astype(B16)
        st = (y[:, :n] * across).astype(B16)
        sc = (z * across).astype(B16)
        at = pl.ds(h, n, stride=heads)
        wide[0][at, :] = _dot(ts, key, 1, 0) + x[:, n:] * lead
        wide[1][at, :] = _dot(st, query, 1, 0) + y[:, n:] * last
        wide[2][at, :] = _dot(
            cat([sc, key * last16], axis=1), cat([grad, state_b], axis=0), 1, 0
        )
    copies = []
    for i, (scr, slab, out) in enumerate(zip(wide, slabs, outs)):
        slab[...] = scr[...].reshape(n, heads, d).astype(B16)
        copy = pltpu.make_async_copy(
            slab, out.at[:, pl.ds(chunk * heads, heads), :], sems.at[i]
        )
        copy.start()
        copies.append(copy)
    for copy in copies:
        copy.wait()


class Plan:
    def __init__(self, seq_size, head_size, n, heads, d, lengths):
        self.n, self.d, self.seq_size, self.head_size = n, d, seq_size, head_size
        self.head_bits, self.seq_bits = _log2(head_size), _log2(seq_size)
        self.levels = self.head_bits + self.seq_bits
        self.scaling = 1.0 / math.sqrt(d * (n * seq_size * head_size // 2))
        self.part = max(heads // CHUNKS, min(heads, head_size))
        self.chunks = heads // self.part
        self.total = heads
        self.lengths = lengths
        device = lax.axis_index("seq") * head_size + lax.axis_index("head")
        device = device.astype(jnp.int32)
        flip = sum(
            ((device >> level) & 1) * (self.part >> (level + 1))
            for level in range(self.head_bits)
        )
        self.place = jnp.stack([device, flip]).astype(jnp.int32)
        self.index = {}
        for level in range(self.levels):
            names = ["up_own", "up_got"]
            if level < self.head_bits:
                names += ["m_in", "m_got", "s_in", "s_own"]
            else:
                names += ["unit"]
            for name in names + (["pick"] if level + 1 == self.levels else []):
                self.index[name, level] = len(self.index)

    def call(self, body, name, ins, in_specs, outs, out_specs, scratch, vmem=VMEM, **kw):
        return pl.pallas_call(
            body,
            in_specs=in_specs,
            out_specs=out_specs,
            out_shape=outs,
            scratch_shapes=scratch,
            compiler_params=pltpu.CompilerParams(vmem_limit_bytes=vmem),
            cost_estimate=pl.CostEstimate(flops=1, bytes_accessed=1, transcendentals=0),
            name=name,
            **kw,
        )(*ins)

    def states(self, chunks, arrays, after):
        n, d, part, count = self.n, self.d, self.part, len(chunks)
        shape = (2, part // 2, d, d)
        first = chunks[0] == 0
        outs = [jax.ShapeDtypeStruct(shape, F32)] * count
        outs += [jax.ShapeDtypeStruct((4, part, n, d), B16)] * count
        outs += [jax.ShapeDtypeStruct((count, *shape), B16)]
        specs = [IN_VMEM] * len(outs)
        if first:
            outs = [jax.ShapeDtypeStruct((2 * len(self.index),), F32)] + outs
            specs = [IN_SMEM] + specs
        got = self.call(
            functools.partial(states_kernel, chunks, self.weights if first else None),
            "states",
            [self.place, self.lengths, *arrays, *after],
            [IN_SMEM] * 2 + [IN_HBM] * 4 + [ANYWHERE] * len(after),
            tuple(outs),
            specs,
            [pltpu.VMEM((count, 4, n, part, d), B16)]
            + [pltpu.VMEM((n * part, d), F32)] * 2
            + [pltpu.SemaphoreType.DMA((count, 4))],
            VMEM_FIRST if first else VMEM_NEXT,
        )
        if first:
            self.scalars, *got = got
        return got[:count], got[count : 2 * count], self.swap(got[-1], 0)

    def grads(self, chunk, heads, mine, got, before, after):
        n, d, part = self.n, self.d, self.part
        out = jax.ShapeDtypeStruct((n, self.total, d), B16)
        return self.call(
            functools.partial(grads_kernel, chunk, self.scaling),
            "grads",
            [self.place, self.lengths, heads, mine, got, *before, *after],
            [IN_SMEM] * 2
            + [IN_VMEM] * 3
            + [IN_HBM] * len(before)
            + [ANYWHERE] * len(after),
            (out, out, out, jax.ShapeDtypeStruct((8, 128), F32)),
            [IN_HBM] * 3 + [IN_VMEM],
            [pltpu.VMEM((n * part, d), F32)] * 3
            + [pltpu.VMEM((n, part, d), B16)] * 3
            + [pltpu.SemaphoreType.DMA((3,))],
            input_output_aliases={5 + i: i for i in range(len(before))},
        )

    def weights(self, place_ref, len_ref, out):
        n, bits = self.n, self.head_bits
        device = place_ref[0]
        begin = ((device >> bits) << bits) * n
        end = begin + (n << bits)
        pairs = []
        for level in range(self.levels):
            group = (device >> (level + 1)) << (level + 1)
            low, high = group * n, (group + (2 << level)) * n
            middle = (group + (1 << level)) * n
            pairs += [(middle - 1, high - 1), (low, middle)]
            if level < bits:
                pairs += [(middle - 1, middle)]
            else:
                pairs += [(middle - 1, begin), (end - 1, middle)]
        same = _same(len_ref, pairs)
        one, zero = F32(1.0), F32(0.0)

        def put(name, level, a, b):
            out[2 * self.index[name, level]] = a
            out[2 * self.index[name, level] + 1] = b

        for level in range(self.levels):
            hi = (device >> level) & 1 == 1
            lasts, firsts = same[0], same[1]
            put("up_own", level, jnp.where(hi, one, lasts), jnp.where(hi, firsts, one))
            put("up_got", level, jnp.where(hi, lasts, one), jnp.where(hi, one, firsts))
            if level < bits:
                join = same[2]
                same = same[3:]
                put("m_in", level, jnp.where(hi, firsts, one), jnp.where(hi, one, lasts))
                put("m_got", level, jnp.where(hi, join, zero), jnp.where(hi, zero, join))
                put("s_in", level, jnp.where(hi, one, firsts), jnp.where(hi, lasts, one))
                put("s_own", level, jnp.where(hi, zero, join), jnp.where(hi, join, zero))
            else:
                ahead, behind = same[2], same[3]
                same = same[4:]
                put("unit", level, jnp.where(hi, ahead, zero), jnp.where(hi, zero, behind))
            if level + 1 == self.levels:
                put("pick", level, jnp.where(hi, zero, one), jnp.where(hi, one, zero))


    def combine(self, name, body, ins, outs, after):
        def kernel(scalar_ref, *refs):
            body(
                lambda name, level, which: scalar_ref[2 * self.index[name, level] + which],
                refs[: len(ins)],
                refs[len(refs) - len(outs) :],
            )

        return self.call(
            kernel,
            name,
            [self.scalars, *ins, *after],
            [IN_SMEM] + [IN_VMEM] * len(ins) + [ANYWHERE] * len(after),
            tuple(outs),
            [IN_VMEM] * len(outs),
            [],
        )

    def order(self):
        bits = self.head_bits
        links = [0] + list(range(1, self.levels)) + list(reversed(range(bits)))
        count = len(links)
        size = max(1, self.chunks // 2)
        step, grads, hop = 1.7, 5.5, [2.0] + [5.4] * (self.levels - 1)
        lasts = [step] * (count - 1) + [grads]
        left = [sum(lasts[i:]) + sum(hop[k] for k in links[i:]) for i in range(count)]

        def run(patience, sign):
            now, free, line = 0.0, [0.0] * self.levels, []
            nexts = [0] * self.chunks
            ready = [-6.0 if chunk < size else 2.0 for chunk in range(self.chunks)]
            while any(i < count for i in nexts):
                open_ = [c for c in range(self.chunks) if nexts[c] < count]

                def rank(c):
                    late = patience if nexts[c] + 1 == count else 0.0
                    return max(now, ready[c] + late), sign * left[nexts[c]], c

                chunk = min(open_, key=rank)
                i = nexts[chunk]
                now = max(now, ready[chunk]) + lasts[i]
                line.append((chunk, i))
                nexts[chunk] += 1
                if i + 1 < count:
                    k = links[i + 1]
                    free[k] = max(now, free[k]) + hop[k]
                    ready[chunk] = free[k]
            return now, line

        tries = [run(p, sign) for sign in (-1.0, 1.0) for p in (0.0, 2.0, 4.0, 8.0, 16.0)]
        return min(tries, key=lambda one: one[0])[1]

    def swap(self, x, level):
        if level < self.head_bits:
            moves = [(i, i ^ (1 << level)) for i in range(self.head_size)]
            return lax.ppermute(x, "head", moves)
        bit = 1 << (level - self.head_bits)
        return lax.ppermute(x, "seq", [(i, i ^ bit) for i in range(self.seq_size)])

    def stages(self, chunk, keep, tokens, swapped, spot):
        d, bits, last = self.d, self.head_bits, self.levels - 1
        own, got, here = [], [], {}

        def shaped(heads, dtype, lead=2):
            return jax.ShapeDtypeStruct((lead, heads, d, d), dtype)

        own.append(keep)
        here["heads"], here["got"] = tokens, swapped

        def up(level, after):
            got.append(here["got"])
            heads = own[-1].shape[1]
            half = heads // 2 if level + 1 < bits else heads
            at = (spot,) if level == 0 else ()

            def body(w, ins, outs):
                for which in range(2):
                    o, g = w("up_own", level, which), w("up_got", level, which)
                    for h in range(heads):
                        x = o * ins[0][which, h] + g * ins[1][(*at, which, h)].astype(F32)
                        if h < half:
                            outs[0][which, h] = x
                        if half == heads:
                            outs[1][which, h] = x.astype(B16)
                        elif h >= half:
                            outs[1][which, h - half] = x.astype(B16)

            outs = [shaped(half, F32), shaped(half, B16)]
            keep, send = self.combine("up", body, [own[-1], got[-1]], outs, after)
            if half < heads:
                own.append(keep)
            else:
                here["total"] = keep
            here["got"] = self.swap(send, level + 1)
            return keep

        def across(level, after):
            ins = [here["total"], here["got"]]
            if "state" in here:
                ins.append(here["state"])
            heads = ins[0].shape[1]
            final = level + 1 == last

            def body(w, ins, outs):
                for h in range(heads):
                    totals = []
                    for which in range(2):
                        other = ins[1][which, h].astype(F32)
                        x = w("up_own", level, which) * ins[0][which, h]
                        x = x + w("up_got", level, which) * other
                        y = w("unit", level, which) * other
                        if len(ins) > 2:
                            y = y + ins[2][which, h]
                        outs[0][which, h] = y
                        totals.append(x)
                        if not final:
                            outs[1][which, h] = x.astype(B16)
                            outs[2][which, h] = x
                    if final:
                        x = w("pick", last, 0) * totals[0] + w("pick", last, 1) * totals[1]
                        outs[1][0, h] = x.astype(B16)

            outs = [shaped(heads, F32), shaped(heads, B16, 1 if final else 2)]
            if not final:
                outs.append(shaped(heads, F32))
            state, send, *total = self.combine("across", body, ins, outs, after)
            here["state"] = state
            here["total"] = total[0] if total else None
            here["got"] = self.swap(send, level + 1)
            return state

        def down(level, after):
            top = level == bits - 1
            ins = [here["state"], here["got"], own[level], got[level]]
            heads = own[level].shape[1]
            half = heads // 2
            factor = self.scaling if level == 0 else 1.0
            at = (spot,) if level == 0 else ()

            def body(w, ins, outs):
                for which in range(2):
                    m_in, m_got, s_in, s_own = (
                        factor * w(name, level, which)
                        for name in ("m_in", "m_got", "s_in", "s_own")
                    )
                    for h in range(heads):
                        if top:
                            x = w("unit", last, which) * ins[1][0, h].astype(F32)
                            x = x + ins[0][which, h]
                        elif h < half:
                            x = ins[0][which, h]
                        else:
                            x = ins[1][which, h - half].astype(F32)
                        mine = m_in * x + m_got * ins[3][(*at, which, h)].astype(F32)
                        theirs = s_in * x + s_own * ins[2][which, h]
                        outs[0][which, h] = mine.astype(outs[0].dtype)
                        outs[1][which, h] = theirs.astype(B16)

            outs = [shaped(heads, B16 if level == 0 else F32), shaped(heads, B16)]
            here["state"], send = self.combine("down", body, ins, outs, after)
            here["got"] = self.swap(send, level)
            return here["state"]

        def final(before, after):
            *outs, token = self.grads(
                chunk, here["heads"], here["state"], here["got"], before, after
            )
            return outs, token

        steps = [functools.partial(up, level) for level in range(bits)]
        steps += [functools.partial(across, level) for level in range(bits, last)]
        steps += [functools.partial(down, level) for level in reversed(range(bits))]
        return steps + [final]


def local(seq_size, head_size, queries, key_heads, value_heads, grad_output, doc_lengths):
    n, heads, d = queries.shape
    arrays = (queries, key_heads, value_heads, grad_output)
    plan = Plan(seq_size, head_size, n, heads, d, doc_lengths)
    stages, after = [], ()
    size = max(1, plan.chunks // 2)
    for begin in range(0, plan.chunks, size):
        chunks = list(range(begin, begin + size))
        keeps, tokens, swapped = plan.states(chunks, arrays, after)
        after = (keeps[0],)
        for spot, chunk in enumerate(chunks):
            stages.append(plan.stages(chunk, keeps[spot], tokens[spot], swapped, spot))
    outs, count = (), len(stages[0])
    for chunk, stage in plan.order():
        if stage + 1 < count:
            after = (stages[chunk][stage](after),)
        else:
            outs, token = stages[chunk][stage](outs, after)
            after = (token,)
    return tuple(outs)


def solution(mesh):
    placed = P(("seq", "head"), None, None)
    return jax.shard_map(
        functools.partial(local, mesh.shape["seq"], mesh.shape["head"]),
        mesh=mesh,
        in_specs=(placed, placed, placed, placed, P()),
        out_specs=(placed, placed, placed),
        check_vma=False,
    )
```

```python
import functools
import math

import jax
import jax.numpy as jnp
from jax import lax
from jax.experimental import pallas as pl
from jax.experimental.pallas import tpu as pltpu
from jax.sharding import PartitionSpec as P

CHUNKS = 4
VMEM = 24 * 1024 * 1024
VMEM_FIRST = 55 * 1024 * 1024
VMEM_NEXT = 46 * 1024 * 1024
F32 = jnp.float32
B16 = jnp.bfloat16
COST = 3690
IN_VMEM = pl.BlockSpec(memory_space=pltpu.VMEM)
IN_SMEM = pl.BlockSpec(memory_space=pltpu.SMEM)
IN_HBM = pl.BlockSpec(memory_space=pltpu.HBM)
ANYWHERE = pl.BlockSpec(memory_space=pl.ANY)


def _log2(n):
    k = n.bit_length() - 1
    assert 1 << k == n
    return k


def _same(len_ref, pairs):
    total = jnp.int32(0)
    split = [jnp.bool_(False)] * len(pairs)
    for k in range(len_ref.shape[0]):
        total = total + len_ref[k]
        split = [s | ((total > p) & (total <= q)) for s, (p, q) in zip(split, pairs)]
    return [jnp.where(s, F32(0.0), F32(1.0)) for s in split]


def _edges(len_ref, first, last):
    start, stop, total = jnp.int32(0), jnp.int32(2**30), jnp.int32(0)
    for k in range(len_ref.shape[0]):
        total = total + len_ref[k]
        start = jnp.where(total <= last, jnp.maximum(start, total), start)
        stop = jnp.where(total > first, jnp.minimum(stop, total), stop)
    return start, stop


def _dot(a, b, ca, cb):
    return lax.dot_general(
        a, b, (((ca,), (cb,)), ((), ())), preferred_element_type=F32
    )


def states_kernel(chunks, weights, place_ref, len_ref, *refs):
    count = len(chunks)
    tokens, refs = refs[:4], refs[len(refs) - 2 * count - (weights is not None) - 5 :]
    if weights is not None:
        scalar_ref, *refs = refs
    keeps, head_refs, send_ref = refs[:count], refs[count : 2 * count], refs[2 * count]
    slab, wide, sems = refs[2 * count + 1], refs[-3:-1], refs[-1]
    n, _, d = tokens[0].shape
    heads = slab.shape[3]
    half = heads // 2
    copies = [
        [
            pltpu.make_async_copy(
                ref.at[:, pl.ds(chunk * heads, heads), :], slab.at[j, i], sems.at[j, i]
            )
            for i, ref in enumerate(tokens)
        ]
        for j, chunk in enumerate(chunks)
    ]
    for some in copies:
        for copy in some:
            copy.start()
    if weights is not None:
        weights(place_ref, len_ref, scalar_ref)
    first = place_ref[0] * n
    flip = place_ref[1]
    start, stop = _edges(len_ref, first, first + n - 1)
    row = lax.broadcasted_iota(jnp.int32, (n, d), 0) + first
    lead = jnp.where(row < stop, F32(1.0), F32(0.0)).astype(B16)
    last = jnp.where(row >= start, F32(1.0), F32(0.0)).astype(B16)
    for j in range(count):
        for i in range(4):
            scr = wide[i % 2]
            copies[j][i].wait()
            scr[...] = slab[j, i].astype(F32).reshape(n * heads, d)
            for h in range(heads):
                head_refs[j][i, h] = scr[pl.ds(h, n, stride=heads), :].astype(B16)
        for r in range(heads):
            h = r ^ flip
            query, key, value, grad = (head_refs[j][i, h] for i in range(4))
            state_a = _dot(key * last, value, 0, 0)
            state_b = _dot(query, grad * lead, 0, 0)
            if r < half:
                keeps[j][0, r] = state_a
                keeps[j][1, r] = state_b
            else:
                send_ref[j, 0, r - half] = state_a.astype(B16)
                send_ref[j, 1, r - half] = state_b.astype(B16)


def grads_kernel(chunk, scaling, place_ref, len_ref, head_ref, mine_ref, *refs):
    got, outs, token_ref = refs[:4], refs[-11:-8], refs[-8]
    wide, slabs, sems = refs[-7:-4], refs[-4:-1], refs[-1]
    token_ref[...] = jnp.zeros(token_ref.shape, token_ref.dtype)
    _, heads, n, d = head_ref.shape
    half = heads // 2
    first = place_ref[0] * n
    flip = place_ref[1]
    start, stop = _edges(len_ref, first, first + n - 1)
    row = lax.broadcasted_iota(jnp.int32, (n, d), 0) + first
    lead = jnp.where(row < stop, F32(1.0), F32(0.0))
    last = jnp.where(row >= start, F32(1.0), F32(0.0))
    last16 = last.astype(B16)

    def live(later):
        t = lax.broadcasted_iota(jnp.int32, (n, n), later) + first
        s = lax.broadcasted_iota(jnp.int32, (n, n), 1 - later) + first
        begin = jnp.zeros((n, n), jnp.int32)
        total = jnp.int32(0)
        for k in range(len_ref.shape[0]):
            total = total + len_ref[k]
            begin = jnp.where(t >= total, total, begin)
        return jnp.where((s <= t) & (s >= begin), F32(scaling), F32(0.0))

    down, across = live(0), live(1)
    cat = jnp.concatenate

    def query_part(query, key, value, grad, state_a, state_b):
        x = _dot(grad, cat([value, state_a], axis=0), 1, 1)
        ts = (x[:, :n] * down).astype(B16)
        return _dot(ts, key, 1, 0) + x[:, n:] * lead

    def key_part(query, key, value, grad, state_a, state_b):
        y = _dot(value, cat([grad, state_b], axis=0), 1, 1)
        st = (y[:, :n] * across).astype(B16)
        return _dot(st, query, 1, 0) + y[:, n:] * last

    def value_part(query, key, value, grad, state_a, state_b):
        sc = (_dot(key, query, 1, 1) * across).astype(B16)
        return _dot(cat([sc, key * last16], axis=1), cat([grad, state_b], axis=0), 1, 0)

    copies = []
    for i, part in enumerate((query_part, key_part, value_part)):
        scr, slab, out = wide[i], slabs[i], outs[i]
        for r in range(heads):
            h = r ^ flip
            if r < half:
                states = mine_ref[0, r], mine_ref[1, r]
            else:
                side, o = divmod(r - half, half // 2)
                states = got[side][0, o], got[2 + side][0, o]
            tokens = [head_ref[a, h] for a in range(4)]
            scr[pl.ds(h, n, stride=heads), :] = part(*tokens, *states)
        slab[...] = scr[...].reshape(n, heads, d).astype(B16)
        copy = pltpu.make_async_copy(
            slab, out.at[:, pl.ds(chunk * heads, heads), :], sems.at[i]
        )
        copy.start()
        copies.append(copy)
    for copy in copies:
        copy.wait()


class Plan:
    def __init__(self, seq_size, head_size, n, heads, d, lengths):
        self.n, self.d, self.seq_size, self.head_size = n, d, seq_size, head_size
        self.head_bits, self.seq_bits = _log2(head_size), _log2(seq_size)
        self.levels = self.head_bits + self.seq_bits
        self.scaling = 1.0 / math.sqrt(d * (n * seq_size * head_size // 2))
        self.part = max(heads // CHUNKS, min(heads, head_size))
        self.chunks = heads // self.part
        self.total = heads
        self.lengths = lengths
        device = lax.axis_index("seq") * head_size + lax.axis_index("head")
        device = device.astype(jnp.int32)
        flip = sum(
            ((device >> level) & 1) * (self.part >> (level + 1))
            for level in range(self.head_bits)
        )
        self.place = jnp.stack([device, flip]).astype(jnp.int32)
        self.index = {}
        for level in range(self.levels):
            names = ["up_own", "up_got"]
            if level < self.head_bits:
                names += ["m_in", "m_got", "s_in", "s_own"]
            else:
                names += ["unit"]
            for name in names + (["pick"] if level + 1 == self.levels else []):
                self.index[name, level] = len(self.index)

    def call(self, body, name, ins, in_specs, outs, out_specs, scratch, vmem=VMEM, cost=700, **kw):
        return pl.pallas_call(
            body,
            in_specs=in_specs,
            out_specs=out_specs,
            out_shape=outs,
            scratch_shapes=scratch,
            compiler_params=pltpu.CompilerParams(vmem_limit_bytes=vmem),
            cost_estimate=pl.CostEstimate(
                flops=1, bytes_accessed=int(cost * COST), transcendentals=0
            ),
            name=name,
            **kw,
        )(*ins)

    def states(self, chunks, arrays, after):
        n, d, part, count = self.n, self.d, self.part, len(chunks)
        shape = (2, part // 2, d, d)
        first = chunks[0] == 0
        outs = [jax.ShapeDtypeStruct(shape, F32)] * count
        outs += [jax.ShapeDtypeStruct((4, part, n, d), B16)] * count
        outs += [jax.ShapeDtypeStruct((count, *shape), B16)]
        specs = [IN_VMEM] * len(outs)
        if first:
            outs = [jax.ShapeDtypeStruct((2 * len(self.index),), F32)] + outs
            specs = [IN_SMEM] + specs
        got = self.call(
            functools.partial(states_kernel, chunks, self.weights if first else None),
            "states",
            [self.place, self.lengths, *arrays, *after],
            [IN_SMEM] * 2 + [IN_HBM] * 4 + [ANYWHERE] * len(after),
            tuple(outs),
            specs,
            [pltpu.VMEM((count, 4, n, part, d), B16)]
            + [pltpu.VMEM((n * part, d), F32)] * 2
            + [pltpu.SemaphoreType.DMA((count, 4))],
            VMEM_FIRST if first else VMEM_NEXT,
            3500 * count,
        )
        if first:
            self.scalars, *got = got
        return got[:count], got[count : 2 * count], self.swap(got[-1], 0)

    def grads(self, chunk, heads, mine, got, before, after):
        n, d, part = self.n, self.d, self.part
        out = jax.ShapeDtypeStruct((n, self.total, d), B16)
        return self.call(
            functools.partial(grads_kernel, chunk, self.scaling),
            "grads",
            [self.place, self.lengths, heads, mine, *got, *before, *after],
            [IN_SMEM] * 2
            + [IN_VMEM] * 6
            + [IN_HBM] * len(before)
            + [ANYWHERE] * len(after),
            (out, out, out, jax.ShapeDtypeStruct((8, 128), F32)),
            [IN_HBM] * 3 + [IN_VMEM],
            [pltpu.VMEM((n * part, d), F32)] * 3
            + [pltpu.VMEM((n, part, d), B16)] * 3
            + [pltpu.SemaphoreType.DMA((3,))],
            cost=5500,
            input_output_aliases={8 + i: i for i in range(len(before))},
        )

    def weights(self, place_ref, len_ref, out):
        n, bits = self.n, self.head_bits
        device = place_ref[0]
        begin = ((device >> bits) << bits) * n
        end = begin + (n << bits)
        pairs = []
        for level in range(self.levels):
            group = (device >> (level + 1)) << (level + 1)
            low, high = group * n, (group + (2 << level)) * n
            middle = (group + (1 << level)) * n
            pairs += [(middle - 1, high - 1), (low, middle)]
            if level < bits:
                pairs += [(middle - 1, middle)]
            else:
                pairs += [(middle - 1, begin), (end - 1, middle)]
        same = _same(len_ref, pairs)
        one, zero = F32(1.0), F32(0.0)

        def put(name, level, a, b):
            out[2 * self.index[name, level]] = a
            out[2 * self.index[name, level] + 1] = b

        for level in range(self.levels):
            hi = (device >> level) & 1 == 1
            lasts, firsts = same[0], same[1]
            put("up_own", level, jnp.where(hi, one, lasts), jnp.where(hi, firsts, one))
            put("up_got", level, jnp.where(hi, lasts, one), jnp.where(hi, one, firsts))
            if level < bits:
                join = same[2]
                same = same[3:]
                put("m_in", level, jnp.where(hi, firsts, one), jnp.where(hi, one, lasts))
                put("m_got", level, jnp.where(hi, join, zero), jnp.where(hi, zero, join))
                put("s_in", level, jnp.where(hi, one, firsts), jnp.where(hi, lasts, one))
                put("s_own", level, jnp.where(hi, zero, join), jnp.where(hi, join, zero))
            else:
                ahead, behind = same[2], same[3]
                same = same[4:]
                put("unit", level, jnp.where(hi, ahead, zero), jnp.where(hi, zero, behind))
            if level + 1 == self.levels:
                put("pick", level, jnp.where(hi, zero, one), jnp.where(hi, one, zero))


    def combine(self, name, body, ins, outs, after):
        def kernel(scalar_ref, *refs):
            body(
                lambda name, level, which: scalar_ref[2 * self.index[name, level] + which],
                refs[: len(ins)],
                refs[len(refs) - len(outs) :],
            )

        return self.call(
            kernel,
            name,
            [self.scalars, *ins, *after],
            [IN_SMEM] + [IN_VMEM] * len(ins) + [ANYWHERE] * len(after),
            tuple(outs),
            [IN_VMEM] * len(outs),
            [],
        )

    def order(self, count):
        chunks = self.chunks
        line = []
        for wave in range(count - 2 + chunks - 1):
            for chunk in reversed(range(chunks)):
                if 0 <= wave - chunk < count - 2:
                    line.append((chunk, wave - chunk))
        fill, final = count - 2, count - 1
        spare = line[-2:] if chunks > 1 else []
        line = line[: len(line) - len(spare)]
        line += [(0, fill), *spare[:-1], (0, final), *spare[-1:]]
        for chunk in range(1, chunks):
            line += [(chunk, fill)] if chunk == 1 else []
            line += [(chunk + 1, fill)] if chunk + 1 < chunks else []
            line.append((chunk, final))
        return line

    def swap(self, x, level):
        if level < self.head_bits:
            moves = [(i, i ^ (1 << level)) for i in range(self.head_size)]
            return lax.ppermute(x, "head", moves)
        bit = 1 << (level - self.head_bits)
        return lax.ppermute(x, "seq", [(i, i ^ bit) for i in range(self.seq_size)])

    def stages(self, chunk, keep, tokens, swapped, spot):
        d, bits, last = self.d, self.head_bits, self.levels - 1
        own, got, here = [], [], {}

        def shaped(heads, dtype, lead=2):
            return jax.ShapeDtypeStruct((lead, heads, d, d), dtype)

        own.append(keep)
        here["heads"], here["got"] = tokens, swapped

        def up(level, after):
            got.append(here["got"])
            heads = own[-1].shape[1]
            half = heads // 2 if level + 1 < bits else heads
            at = (spot,) if level == 0 else ()

            def body(w, ins, outs):
                for which in range(2):
                    o, g = w("up_own", level, which), w("up_got", level, which)
                    for h in range(heads):
                        x = o * ins[0][which, h] + g * ins[1][(*at, which, h)].astype(F32)
                        if h < half:
                            outs[0][which, h] = x
                        if half == heads:
                            outs[1][which, h] = x.astype(B16)
                        elif h >= half:
                            outs[1][which, h - half] = x.astype(B16)

            outs = [shaped(half, F32), shaped(half, B16)]
            keep, send = self.combine("up", body, [own[-1], got[-1]], outs, after)
            if half < heads:
                own.append(keep)
            else:
                here["total"] = keep
            here["got"] = self.swap(send, level + 1)
            return keep

        def across(level, after):
            ins = [here["total"], here["got"]]
            if "state" in here:
                ins.append(here["state"])
            heads = ins[0].shape[1]
            final = level + 1 == last

            def body(w, ins, outs):
                for h in range(heads):
                    totals = []
                    for which in range(2):
                        other = ins[1][which, h].astype(F32)
                        x = w("up_own", level, which) * ins[0][which, h]
                        x = x + w("up_got", level, which) * other
                        y = w("unit", level, which) * other
                        if len(ins) > 2:
                            y = y + ins[2][which, h]
                        outs[0][which, h] = y
                        totals.append(x)
                        if not final:
                            outs[1][which, h] = x.astype(B16)
                            outs[2][which, h] = x
                    if final:
                        x = w("pick", last, 0) * totals[0] + w("pick", last, 1) * totals[1]
                        outs[1][0, h] = x.astype(B16)

            outs = [shaped(heads, F32), shaped(heads, B16, 1 if final else 2)]
            if not final:
                outs.append(shaped(heads, F32))
            state, send, *total = self.combine("across", body, ins, outs, after)
            here["state"] = state
            here["total"] = total[0] if total else None
            here["got"] = self.swap(send, level + 1)
            return state

        def down(level, after):
            top = level == bits - 1
            ins = [here["state"], here["got"], own[level], got[level]]
            heads = own[level].shape[1]
            half = heads // 2
            factor = self.scaling if level == 0 else 1.0
            at = (spot,) if level == 0 else ()

            def body(w, ins, outs):
                for which in range(2):
                    m_in, m_got, s_in, s_own = (
                        factor * w(name, level, which)
                        for name in ("m_in", "m_got", "s_in", "s_own")
                    )
                    for h in range(heads):
                        if top:
                            x = w("unit", last, which) * ins[1][0, h].astype(F32)
                            x = x + ins[0][which, h]
                        elif h < half:
                            x = ins[0][which, h]
                        else:
                            x = ins[1][which, h - half].astype(F32)
                        mine = m_in * x + m_got * ins[3][(*at, which, h)].astype(F32)
                        theirs = s_in * x + s_own * ins[2][which, h]
                        outs[0][which, h] = mine.astype(outs[0].dtype)
                        if level:
                            outs[1][which, h] = theirs.astype(B16)
                        else:
                            outs[1 + 2 * which + h // half][0, h % half] = theirs.astype(B16)

            if level:
                outs = [shaped(heads, F32), shaped(heads, B16)]
            else:
                outs = [shaped(heads, B16)] + [shaped(half, B16, 1)] * 4
            here["state"], *send = self.combine("down", body, ins, outs, after)
            moved = [self.swap(x, level) for x in send]
            here["got"] = moved if level == 0 else moved[0]
            return here["state"]

        def final(before, after):
            *outs, token = self.grads(
                chunk, here["heads"], here["state"], here["got"], before, after
            )
            return outs, token

        steps = [functools.partial(up, level) for level in range(bits)]
        steps += [functools.partial(across, level) for level in range(bits, last)]
        steps += [functools.partial(down, level) for level in reversed(range(bits))]
        return steps + [final]


def local(seq_size, head_size, queries, key_heads, value_heads, grad_output, doc_lengths):
    n, heads, d = queries.shape
    arrays = (queries, key_heads, value_heads, grad_output)
    plan = Plan(seq_size, head_size, n, heads, d, doc_lengths)
    stages, after = [], ()
    size = max(1, plan.chunks // 2)
    for begin in range(0, plan.chunks, size):
        chunks = list(range(begin, begin + size))
        keeps, tokens, swapped = plan.states(chunks, arrays, after)
        after = (keeps[0],)
        for spot, chunk in enumerate(chunks):
            stages.append(plan.stages(chunk, keeps[spot], tokens[spot], swapped, spot))
    outs, count = (), len(stages[0])
    for chunk, stage in plan.order(count):
        if stage + 1 < count:
            after = (stages[chunk][stage](after),)
        else:
            outs, token = stages[chunk][stage](outs, after)
            after = (token,)
    return tuple(outs)


def solution(mesh):
    placed = P(("seq", "head"), None, None)
    return jax.shard_map(
        functools.partial(local, mesh.shape["seq"], mesh.shape["head"]),
        mesh=mesh,
        in_specs=(placed, placed, placed, placed, P()),
        out_specs=(placed, placed, placed),
        check_vma=False,
    )
```

```python
import functools
import math

import jax
import jax.numpy as jnp
from jax import lax
from jax.experimental import pallas as pl
from jax.experimental.pallas import tpu as pltpu
from jax.sharding import PartitionSpec as P

CHUNKS = 4
VMEM = 24 * 1024 * 1024
VMEM_FIRST = 55 * 1024 * 1024
VMEM_NEXT = 46 * 1024 * 1024
F32 = jnp.float32
B16 = jnp.bfloat16
COST = 3690
IN_VMEM = pl.BlockSpec(memory_space=pltpu.VMEM)
IN_SMEM = pl.BlockSpec(memory_space=pltpu.SMEM)
IN_HBM = pl.BlockSpec(memory_space=pltpu.HBM)
ANYWHERE = pl.BlockSpec(memory_space=pl.ANY)


def _log2(n):
    k = n.bit_length() - 1
    assert 1 << k == n
    return k


def _same(len_ref, pairs):
    total = jnp.int32(0)
    split = [jnp.bool_(False)] * len(pairs)
    for k in range(len_ref.shape[0]):
        total = total + len_ref[k]
        split = [s | ((total > p) & (total <= q)) for s, (p, q) in zip(split, pairs)]
    return [jnp.where(s, F32(0.0), F32(1.0)) for s in split]


def _edges(len_ref, first, last):
    start, stop, total = jnp.int32(0), jnp.int32(2**30), jnp.int32(0)
    for k in range(len_ref.shape[0]):
        total = total + len_ref[k]
        start = jnp.where(total <= last, jnp.maximum(start, total), start)
        stop = jnp.where(total > first, jnp.minimum(stop, total), stop)
    return start, stop


def _dot(a, b, ca, cb):
    return lax.dot_general(
        a, b, (((ca,), (cb,)), ((), ())), preferred_element_type=F32
    )


def states_kernel(chunks, weights, place_ref, len_ref, *refs):
    count = len(chunks)
    tokens, refs = refs[:4], refs[len(refs) - 2 * count - (weights is not None) - 5 :]
    if weights is not None:
        scalar_ref, *refs = refs
    keeps, head_refs, send_ref = refs[:count], refs[count : 2 * count], refs[2 * count]
    slab, wide, sems = refs[2 * count + 1], refs[-3:-1], refs[-1]
    n, _, d = tokens[0].shape
    heads = slab.shape[3]
    half = heads // 2
    copies = [
        [
            pltpu.make_async_copy(
                ref.at[:, pl.ds(chunk * heads, heads), :], slab.at[j, i], sems.at[j, i]
            )
            for i, ref in enumerate(tokens)
        ]
        for j, chunk in enumerate(chunks)
    ]
    for some in copies:
        for copy in some:
            copy.start()
    if weights is not None:
        weights(place_ref, len_ref, scalar_ref)
    first = place_ref[0] * n
    flip = place_ref[1]
    start, stop = _edges(len_ref, first, first + n - 1)
    row = lax.broadcasted_iota(jnp.int32, (n, d), 0) + first
    lead = jnp.where(row < stop, F32(1.0), F32(0.0)).astype(B16)
    last = jnp.where(row >= start, F32(1.0), F32(0.0)).astype(B16)
    for j in range(count):
        for i in range(4):
            scr = wide[i % 2]
            copies[j][i].wait()
            scr[...] = slab[j, i].astype(F32).reshape(n * heads, d)
            for h in range(heads):
                head_refs[j][i, h] = scr[pl.ds(h, n, stride=heads), :].astype(B16)
        for r in range(heads):
            h = r ^ flip
            query, key, value, grad = (head_refs[j][i, h] for i in range(4))
            state_a = _dot(key * last, value, 0, 0)
            state_b = _dot(query, grad * lead, 0, 0)
            if r < half:
                keeps[j][0, r] = state_a
                keeps[j][1, r] = state_b
            else:
                send_ref[j, 0, r - half] = state_a.astype(B16)
                send_ref[j, 1, r - half] = state_b.astype(B16)


def _live(len_ref, first, n, scaling, later):
    t = lax.broadcasted_iota(jnp.int32, (n, n), later) + first
    s = lax.broadcasted_iota(jnp.int32, (n, n), 1 - later) + first
    begin = jnp.zeros((n, n), jnp.int32)
    total = jnp.int32(0)
    for k in range(len_ref.shape[0]):
        total = total + len_ref[k]
        begin = jnp.where(t >= total, total, begin)
    return jnp.where((s <= t) & (s >= begin), F32(scaling), F32(0.0))


def inner_kernel(scaling, place_ref, len_ref, head_ref, *refs):
    out = refs[-1]
    _, heads, n, d = head_ref.shape
    first = place_ref[0] * n
    down = _live(len_ref, first, n, scaling, 0)
    across = _live(len_ref, first, n, scaling, 1)
    for h in range(heads):
        query, key, value, grad = (head_ref[i, h] for i in range(4))
        ts = (_dot(grad, value, 1, 1) * down).astype(B16)
        st = (_dot(value, grad, 1, 1) * across).astype(B16)
        sc = (_dot(key, query, 1, 1) * across).astype(B16)
        out[0, h] = _dot(ts, key, 1, 0)
        out[1, h] = _dot(st, query, 1, 0)
        out[2, h] = _dot(sc, grad, 1, 0)


def grads_kernel(chunk, scaling, early, place_ref, len_ref, head_ref, mine_ref, *refs):
    got, outs, token_ref = refs[:4], refs[-11:-8], refs[-8]
    inner_ref = refs[4] if early else None
    wide, slabs, sems = refs[-7:-4], refs[-4:-1], refs[-1]
    token_ref[...] = jnp.zeros(token_ref.shape, token_ref.dtype)
    _, heads, n, d = head_ref.shape
    half = heads // 2
    first = place_ref[0] * n
    flip = place_ref[1]
    start, stop = _edges(len_ref, first, first + n - 1)
    row = lax.broadcasted_iota(jnp.int32, (n, d), 0) + first
    lead = jnp.where(row < stop, F32(1.0), F32(0.0))
    last = jnp.where(row >= start, F32(1.0), F32(0.0))
    last16 = last.astype(B16)
    cat = jnp.concatenate
    if not early:
        down = _live(len_ref, first, n, scaling, 0)
        across = _live(len_ref, first, n, scaling, 1)
    for r in range(heads):
        h = r ^ flip
        if r < half:
            state_a, state_b = mine_ref[0, r], mine_ref[1, r]
        else:
            side, o = divmod(r - half, half // 2)
            state_a, state_b = got[side][0, o], got[2 + side][0, o]
        query, key, value, grad = (head_ref[i, h] for i in range(4))
        at = pl.ds(h, n, stride=heads)
        if early:
            wide[0][at, :] = inner_ref[0, h] + _dot(grad, state_a, 1, 1) * lead
            wide[1][at, :] = inner_ref[1, h] + _dot(value, state_b, 1, 1) * last
            wide[2][at, :] = inner_ref[2, h] + _dot(key, state_b, 1, 0) * last
        else:
            x = _dot(grad, cat([value, state_a], axis=0), 1, 1)
            y = _dot(value, cat([grad, state_b], axis=0), 1, 1)
            z = _dot(key, query, 1, 1)
            ts = (x[:, :n] * down).astype(B16)
            st = (y[:, :n] * across).astype(B16)
            sc = (z * across).astype(B16)
            wide[0][at, :] = _dot(ts, key, 1, 0) + x[:, n:] * lead
            wide[1][at, :] = _dot(st, query, 1, 0) + y[:, n:] * last
            wide[2][at, :] = _dot(
                cat([sc, key * last16], axis=1), cat([grad, state_b], axis=0), 1, 0
            )
    copies = []
    for i, (scr, slab, out) in enumerate(zip(wide, slabs, outs)):
        slab[...] = scr[...].reshape(n, heads, d).astype(B16)
        copy = pltpu.make_async_copy(
            slab, out.at[:, pl.ds(chunk * heads, heads), :], sems.at[i]
        )
        copy.start()
        copies.append(copy)
    for copy in copies:
        copy.wait()


class Plan:
    def __init__(self, seq_size, head_size, n, heads, d, lengths):
        self.n, self.d, self.seq_size, self.head_size = n, d, seq_size, head_size
        self.head_bits, self.seq_bits = _log2(head_size), _log2(seq_size)
        self.levels = self.head_bits + self.seq_bits
        self.scaling = 1.0 / math.sqrt(d * (n * seq_size * head_size // 2))
        self.part = max(heads // CHUNKS, min(heads, head_size))
        self.chunks = heads // self.part
        self.total = heads
        self.lengths = lengths
        device = lax.axis_index("seq") * head_size + lax.axis_index("head")
        device = device.astype(jnp.int32)
        flip = sum(
            ((device >> level) & 1) * (self.part >> (level + 1))
            for level in range(self.head_bits)
        )
        self.place = jnp.stack([device, flip]).astype(jnp.int32)
        self.index, self.early = {}, {}
        for level in range(self.levels):
            names = ["up_own", "up_got"]
            if level < self.head_bits:
                names += ["m_in", "m_got", "s_in", "s_own"]
            else:
                names += ["unit"]
            for name in names + (["pick"] if level + 1 == self.levels else []):
                self.index[name, level] = len(self.index)

    def call(self, body, name, ins, in_specs, outs, out_specs, scratch, vmem=VMEM, cost=700, **kw):
        return pl.pallas_call(
            body,
            in_specs=in_specs,
            out_specs=out_specs,
            out_shape=outs,
            scratch_shapes=scratch,
            compiler_params=pltpu.CompilerParams(vmem_limit_bytes=vmem),
            cost_estimate=pl.CostEstimate(
                flops=1, bytes_accessed=int(cost * COST), transcendentals=0
            ),
            name=name,
            **kw,
        )(*ins)

    def states(self, chunks, arrays, after):
        n, d, part, count = self.n, self.d, self.part, len(chunks)
        shape = (2, part // 2, d, d)
        first = chunks[0] == 0
        outs = [jax.ShapeDtypeStruct(shape, F32)] * count
        outs += [jax.ShapeDtypeStruct((4, part, n, d), B16)] * count
        outs += [jax.ShapeDtypeStruct((count, *shape), B16)]
        specs = [IN_VMEM] * len(outs)
        if first:
            outs = [jax.ShapeDtypeStruct((2 * len(self.index),), F32)] + outs
            specs = [IN_SMEM] + specs
        got = self.call(
            functools.partial(states_kernel, chunks, self.weights if first else None),
            "states",
            [self.place, self.lengths, *arrays, *after],
            [IN_SMEM] * 2 + [IN_HBM] * 4 + [ANYWHERE] * len(after),
            tuple(outs),
            specs,
            [pltpu.VMEM((count, 4, n, part, d), B16)]
            + [pltpu.VMEM((n * part, d), F32)] * 2
            + [pltpu.SemaphoreType.DMA((count, 4))],
            VMEM_FIRST if first else VMEM_NEXT,
            3500 * count,
        )
        if first:
            self.scalars, *got = got
        return got[:count], got[count : 2 * count], self.swap(got[-1], 0)

    def inner(self, heads, after):
        return self.call(
            functools.partial(inner_kernel, self.scaling),
            "inner",
            [self.place, self.lengths, heads, *after],
            [IN_SMEM] * 2 + [IN_VMEM] + [ANYWHERE] * len(after),
            jax.ShapeDtypeStruct((3, self.part, self.n, self.d), F32),
            IN_VMEM,
            [],
        )

    def grads(self, chunk, heads, mine, got, inner, before, after):
        n, d, part = self.n, self.d, self.part
        out = jax.ShapeDtypeStruct((n, self.total, d), B16)
        return self.call(
            functools.partial(grads_kernel, chunk, self.scaling, len(inner) > 0),
            "grads",
            [self.place, self.lengths, heads, mine, *got, *inner, *before, *after],
            [IN_SMEM] * 2
            + [IN_VMEM] * (6 + len(inner))
            + [IN_HBM] * len(before)
            + [ANYWHERE] * len(after),
            (out, out, out, jax.ShapeDtypeStruct((8, 128), F32)),
            [IN_HBM] * 3 + [IN_VMEM],
            [pltpu.VMEM((n * part, d), F32)] * 3
            + [pltpu.VMEM((n, part, d), B16)] * 3
            + [pltpu.SemaphoreType.DMA((3,))],
            input_output_aliases={8 + len(inner) + i: i for i in range(len(before))},
        )

    def weights(self, place_ref, len_ref, out):
        n, bits = self.n, self.head_bits
        device = place_ref[0]
        begin = ((device >> bits) << bits) * n
        end = begin + (n << bits)
        pairs = []
        for level in range(self.levels):
            group = (device >> (level + 1)) << (level + 1)
            low, high = group * n, (group + (2 << level)) * n
            middle = (group + (1 << level)) * n
            pairs += [(middle - 1, high - 1), (low, middle)]
            if level < bits:
                pairs += [(middle - 1, middle)]
            else:
                pairs += [(middle - 1, begin), (end - 1, middle)]
        same = _same(len_ref, pairs)
        one, zero = F32(1.0), F32(0.0)

        def put(name, level, a, b):
            out[2 * self.index[name, level]] = a
            out[2 * self.index[name, level] + 1] = b

        for level in range(self.levels):
            hi = (device >> level) & 1 == 1
            lasts, firsts = same[0], same[1]
            put("up_own", level, jnp.where(hi, one, lasts), jnp.where(hi, firsts, one))
            put("up_got", level, jnp.where(hi, lasts, one), jnp.where(hi, one, firsts))
            if level < bits:
                join = same[2]
                same = same[3:]
                put("m_in", level, jnp.where(hi, firsts, one), jnp.where(hi, one, lasts))
                put("m_got", level, jnp.where(hi, join, zero), jnp.where(hi, zero, join))
                put("s_in", level, jnp.where(hi, one, firsts), jnp.where(hi, lasts, one))
                put("s_own", level, jnp.where(hi, zero, join), jnp.where(hi, join, zero))
            else:
                ahead, behind = same[2], same[3]
                same = same[4:]
                put("unit", level, jnp.where(hi, ahead, zero), jnp.where(hi, zero, behind))
            if level + 1 == self.levels:
                put("pick", level, jnp.where(hi, zero, one), jnp.where(hi, one, zero))


    def combine(self, name, body, ins, outs, after):
        def kernel(scalar_ref, *refs):
            body(
                lambda name, level, which: scalar_ref[2 * self.index[name, level] + which],
                refs[: len(ins)],
                refs[len(refs) - len(outs) :],
            )

        return self.call(
            kernel,
            name,
            [self.scalars, *ins, *after],
            [IN_SMEM] + [IN_VMEM] * len(ins) + [ANYWHERE] * len(after),
            tuple(outs),
            [IN_VMEM] * len(outs),
            [],
        )

    def order(self, count):
        chunks = self.chunks
        line = []
        for wave in range(count - 2 + chunks - 1):
            for chunk in reversed(range(chunks)):
                if 0 <= wave - chunk < count - 2:
                    line.append((chunk, wave - chunk))
        fill, final = count - 2, count - 1
        spare = line[-2:] if chunks > 1 else []
        line = line[: len(line) - len(spare)]
        line += [(0, fill), *spare[:-1], (0, final), *spare[-1:]]
        if chunks > 2:
            line.insert(2, (0, -1))
            line.insert(len(line) - 6, (1, -1))
        for chunk in range(1, chunks):
            line += [(chunk, fill)] if chunk == 1 else []
            line += [(chunk + 1, fill)] if chunk + 1 < chunks else []
            line.append((chunk, final))
        return line

    def swap(self, x, level):
        if level < self.head_bits:
            moves = [(i, i ^ (1 << level)) for i in range(self.head_size)]
            return lax.ppermute(x, "head", moves)
        bit = 1 << (level - self.head_bits)
        return lax.ppermute(x, "seq", [(i, i ^ bit) for i in range(self.seq_size)])

    def stages(self, chunk, keep, tokens, swapped, spot):
        d, bits, last = self.d, self.head_bits, self.levels - 1
        own, got, here = [], [], {}

        def shaped(heads, dtype, lead=2):
            return jax.ShapeDtypeStruct((lead, heads, d, d), dtype)

        own.append(keep)
        here["heads"], here["got"] = tokens, swapped

        def up(level, after):
            got.append(here["got"])
            heads = own[-1].shape[1]
            half = heads // 2 if level + 1 < bits else heads
            at = (spot,) if level == 0 else ()

            def body(w, ins, outs):
                for which in range(2):
                    o, g = w("up_own", level, which), w("up_got", level, which)
                    for h in range(heads):
                        x = o * ins[0][which, h] + g * ins[1][(*at, which, h)].astype(F32)
                        if h < half:
                            outs[0][which, h] = x
                        if half == heads:
                            outs[1][which, h] = x.astype(B16)
                        elif h >= half:
                            outs[1][which, h - half] = x.astype(B16)

            outs = [shaped(half, F32), shaped(half, B16)]
            keep, send = self.combine("up", body, [own[-1], got[-1]], outs, after)
            if half < heads:
                own.append(keep)
            else:
                here["total"] = keep
            here["got"] = self.swap(send, level + 1)
            return keep

        def across(level, after):
            ins = [here["total"], here["got"]]
            if "state" in here:
                ins.append(here["state"])
            heads = ins[0].shape[1]
            final = level + 1 == last

            def body(w, ins, outs):
                for h in range(heads):
                    totals = []
                    for which in range(2):
                        other = ins[1][which, h].astype(F32)
                        x = w("up_own", level, which) * ins[0][which, h]
                        x = x + w("up_got", level, which) * other
                        y = w("unit", level, which) * other
                        if len(ins) > 2:
                            y = y + ins[2][which, h]
                        outs[0][which, h] = y
                        totals.append(x)
                        if not final:
                            outs[1][which, h] = x.astype(B16)
                            outs[2][which, h] = x
                    if final:
                        x = w("pick", last, 0) * totals[0] + w("pick", last, 1) * totals[1]
                        outs[1][0, h] = x.astype(B16)

            outs = [shaped(heads, F32), shaped(heads, B16, 1 if final else 2)]
            if not final:
                outs.append(shaped(heads, F32))
            state, send, *total = self.combine("across", body, ins, outs, after)
            here["state"] = state
            here["total"] = total[0] if total else None
            here["got"] = self.swap(send, level + 1)
            return state

        def down(level, after):
            top = level == bits - 1
            ins = [here["state"], here["got"], own[level], got[level]]
            heads = own[level].shape[1]
            half = heads // 2
            factor = self.scaling if level == 0 else 1.0
            at = (spot,) if level == 0 else ()

            def body(w, ins, outs):
                for which in range(2):
                    m_in, m_got, s_in, s_own = (
                        factor * w(name, level, which)
                        for name in ("m_in", "m_got", "s_in", "s_own")
                    )
                    for h in range(heads):
                        if top:
                            x = w("unit", last, which) * ins[1][0, h].astype(F32)
                            x = x + ins[0][which, h]
                        elif h < half:
                            x = ins[0][which, h]
                        else:
                            x = ins[1][which, h - half].astype(F32)
                        mine = m_in * x + m_got * ins[3][(*at, which, h)].astype(F32)
                        theirs = s_in * x + s_own * ins[2][which, h]
                        outs[0][which, h] = mine.astype(outs[0].dtype)
                        if level:
                            outs[1][which, h] = theirs.astype(B16)
                        else:
                            outs[1 + 2 * which + h // half][0, h % half] = theirs.astype(B16)

            if level:
                outs = [shaped(heads, F32), shaped(heads, B16)]
            else:
                outs = [shaped(heads, B16)] + [shaped(half, B16, 1)] * 4
            here["state"], *send = self.combine("down", body, ins, outs, after)
            moved = [self.swap(x, level) for x in send]
            here["got"] = moved if level == 0 else moved[0]
            return here["state"]

        def final(before, after):
            *outs, token = self.grads(
                chunk, here["heads"], here["state"], here["got"], here["inner"], before, after
            )
            return outs, token

        def early(after):
            here["inner"] = (self.inner(here["heads"], after),)
            return here["inner"][0]

        here["inner"] = ()
        self.early[chunk] = early
        steps = [functools.partial(up, level) for level in range(bits)]
        steps += [functools.partial(across, level) for level in range(bits, last)]
        steps += [functools.partial(down, level) for level in reversed(range(bits))]
        return steps + [final]


def local(seq_size, head_size, queries, key_heads, value_heads, grad_output, doc_lengths):
    n, heads, d = queries.shape
    arrays = (queries, key_heads, value_heads, grad_output)
    plan = Plan(seq_size, head_size, n, heads, d, doc_lengths)
    stages, after = [], ()
    size = max(1, plan.chunks // 2)
    for begin in range(0, plan.chunks, size):
        chunks = list(range(begin, begin + size))
        keeps, tokens, swapped = plan.states(chunks, arrays, after)
        after = (keeps[0],)
        for spot, chunk in enumerate(chunks):
            stages.append(plan.stages(chunk, keeps[spot], tokens[spot], swapped, spot))
    outs, count = (), len(stages[0])
    for chunk, stage in plan.order(count):
        if stage < 0:
            after = (plan.early[chunk](after),)
        elif stage + 1 < count:
            after = (stages[chunk][stage](after),)
        else:
            outs, token = stages[chunk][stage](outs, after)
            after = (token,)
    return tuple(outs)


def solution(mesh):
    placed = P(("seq", "head"), None, None)
    return jax.shard_map(
        functools.partial(local, mesh.shape["seq"], mesh.shape["head"]),
        mesh=mesh,
        in_specs=(placed, placed, placed, placed, P()),
        out_specs=(placed, placed, placed),
        check_vma=False,
    )
```

```python
import functools
import math

import jax
import jax.numpy as jnp
from jax import lax
from jax.experimental import pallas as pl
from jax.experimental.pallas import tpu as pltpu
from jax.sharding import PartitionSpec as P

CHUNKS = 4
VMEM = 24 * 1024 * 1024
VMEM_FIRST = 55 * 1024 * 1024
VMEM_NEXT = 46 * 1024 * 1024
F32 = jnp.float32
B16 = jnp.bfloat16
COST = 3690
IN_VMEM = pl.BlockSpec(memory_space=pltpu.VMEM)
IN_SMEM = pl.BlockSpec(memory_space=pltpu.SMEM)
IN_HBM = pl.BlockSpec(memory_space=pltpu.HBM)
ANYWHERE = pl.BlockSpec(memory_space=pl.ANY)


def _log2(n):
    k = n.bit_length() - 1
    assert 1 << k == n
    return k


def _same(len_ref, pairs):
    total = jnp.int32(0)
    split = [jnp.bool_(False)] * len(pairs)
    for k in range(len_ref.shape[0]):
        total = total + len_ref[k]
        split = [s | ((total > p) & (total <= q)) for s, (p, q) in zip(split, pairs)]
    return [jnp.where(s, F32(0.0), F32(1.0)) for s in split]


def _edges(len_ref, first, last):
    start, stop, total = jnp.int32(0), jnp.int32(2**30), jnp.int32(0)
    for k in range(len_ref.shape[0]):
        total = total + len_ref[k]
        start = jnp.where(total <= last, jnp.maximum(start, total), start)
        stop = jnp.where(total > first, jnp.minimum(stop, total), stop)
    return start, stop


def _dot(a, b, ca, cb):
    return lax.dot_general(
        a, b, (((ca,), (cb,)), ((), ())), preferred_element_type=F32
    )


def states_kernel(chunks, weights, place_ref, len_ref, *refs):
    count = len(chunks)
    tokens, refs = refs[:4], refs[len(refs) - 4 * count - (weights is not None) - 4 :]
    if weights is not None:
        scalar_ref, *refs = refs
    keeps, head_refs = refs[:count], refs[count : 2 * count]
    sends = refs[2 * count : 4 * count]
    slab, wide, sems = refs[-4], refs[-3:-1], refs[-1]
    n, _, d = tokens[0].shape
    heads = slab.shape[3]
    half = heads // 2
    copies = [
        [
            pltpu.make_async_copy(
                ref.at[:, pl.ds(chunk * heads, heads), :], slab.at[j, i], sems.at[j, i]
            )
            for i, ref in enumerate(tokens)
        ]
        for j, chunk in enumerate(chunks)
    ]
    for some in copies:
        for copy in some:
            copy.start()
    if weights is not None:
        weights(place_ref, len_ref, scalar_ref)
    first = place_ref[0] * n
    flip = place_ref[1]
    start, stop = _edges(len_ref, first, first + n - 1)
    row = lax.broadcasted_iota(jnp.int32, (n, d), 0) + first
    lead = jnp.where(row < stop, F32(1.0), F32(0.0)).astype(B16)
    last = jnp.where(row >= start, F32(1.0), F32(0.0)).astype(B16)
    for j in range(count):
        for i in range(4):
            scr = wide[i % 2]
            copies[j][i].wait()
            scr[...] = slab[j, i].astype(F32).reshape(n * heads, d)
            for h in range(heads):
                head_refs[j][i, h] = scr[pl.ds(h, n, stride=heads), :].astype(B16)
        for r in range(heads):
            h = r ^ flip
            query, key, value, grad = (head_refs[j][i, h] for i in range(4))
            state_a = _dot(key * last, value, 0, 0)
            state_b = _dot(query, grad * lead, 0, 0)
            if r < half:
                keeps[j][0, r] = state_a
                keeps[j][1, r] = state_b
            else:
                sends[2 * j][0, r - half] = state_a.astype(B16)
                sends[2 * j + 1][0, r - half] = state_b.astype(B16)


def _live(len_ref, first, n, scaling, later):
    t = lax.broadcasted_iota(jnp.int32, (n, n), later) + first
    s = lax.broadcasted_iota(jnp.int32, (n, n), 1 - later) + first
    begin = jnp.zeros((n, n), jnp.int32)
    total = jnp.int32(0)
    for k in range(len_ref.shape[0]):
        total = total + len_ref[k]
        begin = jnp.where(t >= total, total, begin)
    return jnp.where((s <= t) & (s >= begin), F32(scaling), F32(0.0))


def inner_kernel(scaling, place_ref, len_ref, head_ref, *refs):
    out = refs[-1]
    _, heads, n, d = head_ref.shape
    first = place_ref[0] * n
    down = _live(len_ref, first, n, scaling, 0)
    across = _live(len_ref, first, n, scaling, 1)
    for h in range(heads):
        query, key, value, grad = (head_ref[i, h] for i in range(4))
        ts = (_dot(grad, value, 1, 1) * down).astype(B16)
        st = (_dot(value, grad, 1, 1) * across).astype(B16)
        sc = (_dot(key, query, 1, 1) * across).astype(B16)
        out[0, h] = _dot(ts, key, 1, 0)
        out[1, h] = _dot(st, query, 1, 0)
        out[2, h] = _dot(sc, grad, 1, 0)


def grads_kernel(chunk, scaling, early, place_ref, len_ref, head_ref, mine_ref, *refs):
    got, outs, token_ref = refs[:4], refs[-11:-8], refs[-8]
    inner_ref = refs[4] if early else None
    wide, slabs, sems = refs[-7:-4], refs[-4:-1], refs[-1]
    token_ref[...] = jnp.zeros(token_ref.shape, token_ref.dtype)
    _, heads, n, d = head_ref.shape
    half = heads // 2
    first = place_ref[0] * n
    flip = place_ref[1]
    start, stop = _edges(len_ref, first, first + n - 1)
    row = lax.broadcasted_iota(jnp.int32, (n, d), 0) + first
    lead = jnp.where(row < stop, F32(1.0), F32(0.0))
    last = jnp.where(row >= start, F32(1.0), F32(0.0))
    last16 = last.astype(B16)
    cat = jnp.concatenate
    if not early:
        down = _live(len_ref, first, n, scaling, 0)
        across = _live(len_ref, first, n, scaling, 1)
    for r in range(heads):
        h = r ^ flip
        if r < half:
            state_a, state_b = mine_ref[0, r], mine_ref[1, r]
        else:
            side, o = divmod(r - half, half // 2)
            state_a, state_b = got[side][0, o], got[2 + side][0, o]
        query, key, value, grad = (head_ref[i, h] for i in range(4))
        at = pl.ds(h, n, stride=heads)
        if early:
            wide[0][at, :] = inner_ref[0, h] + _dot(grad, state_a, 1, 1) * lead
            wide[1][at, :] = inner_ref[1, h] + _dot(value, state_b, 1, 1) * last
            wide[2][at, :] = inner_ref[2, h] + _dot(key, state_b, 1, 0) * last
        else:
            x = _dot(grad, cat([value, state_a], axis=0), 1, 1)
            y = _dot(value, cat([grad, state_b], axis=0), 1, 1)
            z = _dot(key, query, 1, 1)
            ts = (x[:, :n] * down).astype(B16)
            st = (y[:, :n] * across).astype(B16)
            sc = (z * across).astype(B16)
            wide[0][at, :] = _dot(ts, key, 1, 0) + x[:, n:] * lead
            wide[1][at, :] = _dot(st, query, 1, 0) + y[:, n:] * last
            wide[2][at, :] = _dot(
                cat([sc, key * last16], axis=1), cat([grad, state_b], axis=0), 1, 0
            )
    copies = []
    for i, (scr, slab, out) in enumerate(zip(wide, slabs, outs)):
        slab[...] = scr[...].reshape(n, heads, d).astype(B16)
        copy = pltpu.make_async_copy(
            slab, out.at[:, pl.ds(chunk * heads, heads), :], sems.at[i]
        )
        copy.start()
        copies.append(copy)
    for copy in copies:
        copy.wait()


class Plan:
    def __init__(self, seq_size, head_size, n, heads, d, lengths):
        self.n, self.d, self.seq_size, self.head_size = n, d, seq_size, head_size
        self.head_bits, self.seq_bits = _log2(head_size), _log2(seq_size)
        self.levels = self.head_bits + self.seq_bits
        self.scaling = 1.0 / math.sqrt(d * (n * seq_size * head_size // 2))
        self.part = max(heads // CHUNKS, min(heads, head_size))
        self.chunks = heads // self.part
        self.total = heads
        self.lengths = lengths
        device = lax.axis_index("seq") * head_size + lax.axis_index("head")
        device = device.astype(jnp.int32)
        flip = sum(
            ((device >> level) & 1) * (self.part >> (level + 1))
            for level in range(self.head_bits)
        )
        self.place = jnp.stack([device, flip]).astype(jnp.int32)
        self.index, self.early = {}, {}
        for level in range(self.levels):
            names = ["up_own", "up_got"]
            if level < self.head_bits:
                names += ["m_in", "m_got", "s_in", "s_own"]
            else:
                names += ["unit"]
            for name in names + (["pick"] if level + 1 == self.levels else []):
                self.index[name, level] = len(self.index)

    def call(self, body, name, ins, in_specs, outs, out_specs, scratch, vmem=VMEM, cost=700, **kw):
        return pl.pallas_call(
            body,
            in_specs=in_specs,
            out_specs=out_specs,
            out_shape=outs,
            scratch_shapes=scratch,
            compiler_params=pltpu.CompilerParams(vmem_limit_bytes=vmem),
            cost_estimate=pl.CostEstimate(
                flops=1, bytes_accessed=int(cost * COST), transcendentals=0
            ),
            name=name,
            **kw,
        )(*ins)

    def states(self, chunks, arrays, after):
        n, d, part, count = self.n, self.d, self.part, len(chunks)
        shape = (2, part // 2, d, d)
        first = chunks[0] == 0
        outs = [jax.ShapeDtypeStruct(shape, F32)] * count
        outs += [jax.ShapeDtypeStruct((4, part, n, d), B16)] * count
        outs += [jax.ShapeDtypeStruct((1, *shape[1:]), B16)] * (2 * count)
        specs = [IN_VMEM] * len(outs)
        if first:
            outs = [jax.ShapeDtypeStruct((2 * len(self.index),), F32)] + outs
            specs = [IN_SMEM] + specs
        got = self.call(
            functools.partial(states_kernel, chunks, self.weights if first else None),
            "states",
            [self.place, self.lengths, *arrays, *after],
            [IN_SMEM] * 2 + [IN_HBM] * 4 + [ANYWHERE] * len(after),
            tuple(outs),
            specs,
            [pltpu.VMEM((count, 4, n, part, d), B16)]
            + [pltpu.VMEM((n * part, d), F32)] * 2
            + [pltpu.SemaphoreType.DMA((count, 4))],
            VMEM_FIRST if first else VMEM_NEXT,
            3500 * count,
        )
        if first:
            self.scalars, *got = got
        moved = [self.swap(x, 0) for x in got[2 * count :]]
        return got[:count], got[count : 2 * count], moved

    def inner(self, heads, after):
        return self.call(
            functools.partial(inner_kernel, self.scaling),
            "inner",
            [self.place, self.lengths, heads, *after],
            [IN_SMEM] * 2 + [IN_VMEM] + [ANYWHERE] * len(after),
            jax.ShapeDtypeStruct((3, self.part, self.n, self.d), F32),
            IN_VMEM,
            [],
        )

    def grads(self, chunk, heads, mine, got, inner, before, after):
        n, d, part = self.n, self.d, self.part
        out = jax.ShapeDtypeStruct((n, self.total, d), B16)
        return self.call(
            functools.partial(grads_kernel, chunk, self.scaling, len(inner) > 0),
            "grads",
            [self.place, self.lengths, heads, mine, *got, *inner, *before, *after],
            [IN_SMEM] * 2
            + [IN_VMEM] * (6 + len(inner))
            + [IN_HBM] * len(before)
            + [ANYWHERE] * len(after),
            (out, out, out, jax.ShapeDtypeStruct((8, 128), F32)),
            [IN_HBM] * 3 + [IN_VMEM],
            [pltpu.VMEM((n * part, d), F32)] * 3
            + [pltpu.VMEM((n, part, d), B16)] * 3
            + [pltpu.SemaphoreType.DMA((3,))],
            input_output_aliases={8 + len(inner) + i: i for i in range(len(before))},
        )

    def weights(self, place_ref, len_ref, out):
        n, bits = self.n, self.head_bits
        device = place_ref[0]
        begin = ((device >> bits) << bits) * n
        end = begin + (n << bits)
        pairs = []
        for level in range(self.levels):
            group = (device >> (level + 1)) << (level + 1)
            low, high = group * n, (group + (2 << level)) * n
            middle = (group + (1 << level)) * n
            pairs += [(middle - 1, high - 1), (low, middle)]
            if level < bits:
                pairs += [(middle - 1, middle)]
            else:
                pairs += [(middle - 1, begin), (end - 1, middle)]
        same = _same(len_ref, pairs)
        one, zero = F32(1.0), F32(0.0)

        def put(name, level, a, b):
            out[2 * self.index[name, level]] = a
            out[2 * self.index[name, level] + 1] = b

        for level in range(self.levels):
            hi = (device >> level) & 1 == 1
            lasts, firsts = same[0], same[1]
            put("up_own", level, jnp.where(hi, one, lasts), jnp.where(hi, firsts, one))
            put("up_got", level, jnp.where(hi, lasts, one), jnp.where(hi, one, firsts))
            if level < bits:
                join = same[2]
                same = same[3:]
                put("m_in", level, jnp.where(hi, firsts, one), jnp.where(hi, one, lasts))
                put("m_got", level, jnp.where(hi, join, zero), jnp.where(hi, zero, join))
                put("s_in", level, jnp.where(hi, one, firsts), jnp.where(hi, lasts, one))
                put("s_own", level, jnp.where(hi, zero, join), jnp.where(hi, join, zero))
            else:
                ahead, behind = same[2], same[3]
                same = same[4:]
                put("unit", level, jnp.where(hi, ahead, zero), jnp.where(hi, zero, behind))
            if level + 1 == self.levels:
                put("pick", level, jnp.where(hi, zero, one), jnp.where(hi, one, zero))


    def combine(self, name, body, ins, outs, after):
        def kernel(scalar_ref, *refs):
            body(
                lambda name, level, which: scalar_ref[2 * self.index[name, level] + which],
                refs[: len(ins)],
                refs[len(refs) - len(outs) :],
            )

        return self.call(
            kernel,
            name,
            [self.scalars, *ins, *after],
            [IN_SMEM] + [IN_VMEM] * len(ins) + [ANYWHERE] * len(after),
            tuple(outs),
            [IN_VMEM] * len(outs),
            [],
        )

    def order(self, count):
        chunks, size = self.chunks, max(1, self.chunks // 2)
        line = [(chunk, 1) for chunk in range(size)]
        line += [(chunk, 0) for chunk in range(size, chunks)]
        for wave in range(count - 2 + chunks - 1):
            for chunk in reversed(range(chunks)):
                one = (chunk, wave - chunk)
                if 0 < one[1] < count - 2 and one not in line:
                    line.append(one)
        fill, final = count - 2, count - 1
        spare = line[-2:] if chunks > 1 else []
        line = line[: len(line) - len(spare)]
        line += [(0, fill), *spare[:-1], (0, final)]
        if chunks > 2:
            line += [(2, -1)]
            line.insert(len(line) - 6, (1, -1))
            line.insert(line.index((0, count - 3)), (0, -1))
        line += spare[-1:]
        for chunk in range(1, chunks):
            line += [(chunk, fill)] if chunk == 1 else []
            line += [(chunk + 1, fill)] if chunk + 1 < chunks else []
            line.append((chunk, final))
        return line

    def swap(self, x, level):
        if level < self.head_bits:
            moves = [(i, i ^ (1 << level)) for i in range(self.head_size)]
            return lax.ppermute(x, "head", moves)
        bit = 1 << (level - self.head_bits)
        return lax.ppermute(x, "seq", [(i, i ^ bit) for i in range(self.seq_size)])

    def stages(self, chunk, keep, tokens, swapped):
        d, bits, last = self.d, self.head_bits, self.levels - 1
        own, got, here = [], [], {}

        def shaped(heads, dtype, lead=2):
            return jax.ShapeDtypeStruct((lead, heads, d, d), dtype)

        own.append(keep)
        here["heads"], here["got"] = tokens, swapped

        def up(level, after):
            got.append(here["got"] if level == 0 else [here["got"]])
            heads = own[-1].shape[1]
            half = heads // 2 if level + 1 < bits else heads

            def body(w, ins, outs):
                for which in range(2):
                    o, g = w("up_own", level, which), w("up_got", level, which)
                    for h in range(heads):
                        other = ins[1][which, h] if level else ins[1 + which][0, h]
                        x = o * ins[0][which, h] + g * other.astype(F32)
                        if h < half:
                            outs[0][which, h] = x
                        if half == heads:
                            outs[1][which, h] = x.astype(B16)
                        elif h >= half:
                            outs[1][which, h - half] = x.astype(B16)

            outs = [shaped(half, F32), shaped(half, B16)]
            keep, send = self.combine("up", body, [own[-1], *got[-1]], outs, after)
            if half < heads:
                own.append(keep)
            else:
                here["total"] = keep
            here["got"] = self.swap(send, level + 1)
            return keep

        def across(level, after):
            ins = [here["total"], here["got"]]
            if "state" in here:
                ins.append(here["state"])
            heads = ins[0].shape[1]
            final = level + 1 == last

            def body(w, ins, outs):
                for h in range(heads):
                    totals = []
                    for which in range(2):
                        other = ins[1][which, h].astype(F32)
                        x = w("up_own", level, which) * ins[0][which, h]
                        x = x + w("up_got", level, which) * other
                        y = w("unit", level, which) * other
                        if len(ins) > 2:
                            y = y + ins[2][which, h]
                        outs[0][which, h] = y
                        totals.append(x)
                        if not final:
                            outs[1][which, h] = x.astype(B16)
                            outs[2][which, h] = x
                    if final:
                        x = w("pick", last, 0) * totals[0] + w("pick", last, 1) * totals[1]
                        outs[1][0, h] = x.astype(B16)

            outs = [shaped(heads, F32), shaped(heads, B16, 1 if final else 2)]
            if not final:
                outs.append(shaped(heads, F32))
            state, send, *total = self.combine("across", body, ins, outs, after)
            here["state"] = state
            here["total"] = total[0] if total else None
            here["got"] = self.swap(send, level + 1)
            return state

        def down(level, after):
            top = level == bits - 1
            ins = [here["state"], here["got"], own[level], *got[level]]
            heads = own[level].shape[1]
            half = heads // 2
            factor = self.scaling if level == 0 else 1.0

            def body(w, ins, outs):
                for which in range(2):
                    m_in, m_got, s_in, s_own = (
                        factor * w(name, level, which)
                        for name in ("m_in", "m_got", "s_in", "s_own")
                    )
                    for h in range(heads):
                        if top:
                            x = w("unit", last, which) * ins[1][0, h].astype(F32)
                            x = x + ins[0][which, h]
                        elif h < half:
                            x = ins[0][which, h]
                        else:
                            x = ins[1][which, h - half].astype(F32)
                        other = ins[3][which, h] if level else ins[3 + which][0, h]
                        mine = m_in * x + m_got * other.astype(F32)
                        theirs = s_in * x + s_own * ins[2][which, h]
                        outs[0][which, h] = mine.astype(outs[0].dtype)
                        if level:
                            outs[1][which, h] = theirs.astype(B16)
                        else:
                            outs[1 + 2 * which + h // half][0, h % half] = theirs.astype(B16)

            if level:
                outs = [shaped(heads, F32), shaped(heads, B16)]
            else:
                outs = [shaped(heads, B16)] + [shaped(half, B16, 1)] * 4
            here["state"], *send = self.combine("down", body, ins, outs, after)
            moved = [self.swap(x, level) for x in send]
            here["got"] = moved if level == 0 else moved[0]
            return here["state"]

        def final(before, after):
            *outs, token = self.grads(
                chunk, here["heads"], here["state"], here["got"], here["inner"], before, after
            )
            return outs, token

        def early(after):
            here["inner"] = (self.inner(here["heads"], after),)
            return here["inner"][0]

        here["inner"] = ()
        self.early[chunk] = early
        steps = [functools.partial(up, level) for level in range(bits)]
        steps += [functools.partial(across, level) for level in range(bits, last)]
        steps += [functools.partial(down, level) for level in reversed(range(bits))]
        return steps + [final]


def local(seq_size, head_size, queries, key_heads, value_heads, grad_output, doc_lengths):
    n, heads, d = queries.shape
    arrays = (queries, key_heads, value_heads, grad_output)
    plan = Plan(seq_size, head_size, n, heads, d, doc_lengths)
    stages, after = [], ()
    size = max(1, plan.chunks // 2)
    for begin in range(0, plan.chunks, size):
        chunks = list(range(begin, begin + size))
        keeps, tokens, moved = plan.states(chunks, arrays, after)
        after = (keeps[0],)
        for spot, chunk in enumerate(chunks):
            swapped = moved[2 * spot : 2 * spot + 2]
            stages.append(plan.stages(chunk, keeps[spot], tokens[spot], swapped))
        if begin == 0:
            for chunk in chunks:
                after = (stages[chunk][0](after),)
    outs, count = (), len(stages[0])
    for chunk, stage in plan.order(count):
        if stage < 0:
            after = (plan.early[chunk](after),)
        elif stage + 1 < count:
            after = (stages[chunk][stage](after),)
        else:
            outs, token = stages[chunk][stage](outs, after)
            after = (token,)
    return tuple(outs)


def solution(mesh):
    placed = P(("seq", "head"), None, None)
    return jax.shard_map(
        functools.partial(local, mesh.shape["seq"], mesh.shape["head"]),
        mesh=mesh,
        in_specs=(placed, placed, placed, placed, P()),
        out_specs=(placed, placed, placed),
        check_vma=False,
    )
```

```python
import functools
import math

import jax
import jax.numpy as jnp
from jax import lax
from jax.experimental import pallas as pl
from jax.experimental.pallas import tpu as pltpu
from jax.sharding import PartitionSpec as P

CHUNKS = 4
VMEM = 24 * 1024 * 1024
VMEM_FIRST = 55 * 1024 * 1024
VMEM_NEXT = 46 * 1024 * 1024
F32 = jnp.float32
B16 = jnp.bfloat16
COST = 3690
IN_VMEM = pl.BlockSpec(memory_space=pltpu.VMEM)
IN_SMEM = pl.BlockSpec(memory_space=pltpu.SMEM)
IN_HBM = pl.BlockSpec(memory_space=pltpu.HBM)
ANYWHERE = pl.BlockSpec(memory_space=pl.ANY)


def _log2(n):
    k = n.bit_length() - 1
    assert 1 << k == n
    return k


def _same(len_ref, pairs):
    total = jnp.int32(0)
    split = [jnp.bool_(False)] * len(pairs)
    for k in range(len_ref.shape[0]):
        total = total + len_ref[k]
        split = [s | ((total > p) & (total <= q)) for s, (p, q) in zip(split, pairs)]
    return [jnp.where(s, F32(0.0), F32(1.0)) for s in split]


def _edges(len_ref, first, last):
    start, stop, total = jnp.int32(0), jnp.int32(2**30), jnp.int32(0)
    for k in range(len_ref.shape[0]):
        total = total + len_ref[k]
        start = jnp.where(total <= last, jnp.maximum(start, total), start)
        stop = jnp.where(total > first, jnp.minimum(stop, total), stop)
    return start, stop


def _dot(a, b, ca, cb):
    return lax.dot_general(
        a, b, (((ca,), (cb,)), ((), ())), preferred_element_type=F32
    )


def states_kernel(chunks, weights, place_ref, len_ref, *refs):
    count = len(chunks)
    tokens, refs = refs[:4], refs[len(refs) - 4 * count - (weights is not None) - 4 :]
    if weights is not None:
        scalar_ref, *refs = refs
    keeps, head_refs = refs[:count], refs[count : 2 * count]
    sends = refs[2 * count : 4 * count]
    slab, wide, sems = refs[-4], refs[-3:-1], refs[-1]
    n, _, d = tokens[0].shape
    heads = slab.shape[3]
    half = heads // 2
    copies = [
        [
            pltpu.make_async_copy(
                ref.at[:, pl.ds(chunk * heads, heads), :], slab.at[j, i], sems.at[j, i]
            )
            for i, ref in enumerate(tokens)
        ]
        for j, chunk in enumerate(chunks)
    ]
    for some in copies:
        for copy in some:
            copy.start()
    if weights is not None:
        weights(place_ref, len_ref, scalar_ref)
    first = place_ref[0] * n
    flip = place_ref[1]
    start, stop = _edges(len_ref, first, first + n - 1)
    row = lax.broadcasted_iota(jnp.int32, (n, d), 0) + first
    lead = jnp.where(row < stop, F32(1.0), F32(0.0)).astype(B16)
    last = jnp.where(row >= start, F32(1.0), F32(0.0)).astype(B16)
    for j in range(count):
        for i in range(4):
            scr = wide[i % 2]
            copies[j][i].wait()
            scr[...] = slab[j, i].astype(F32).reshape(n * heads, d)
            for h in range(heads):
                head_refs[j][i, h] = scr[pl.ds(h, n, stride=heads), :].astype(B16)
        for r in range(heads):
            h = r ^ flip
            query, key, value, grad = (head_refs[j][i, h] for i in range(4))
            state_a = _dot(key * last, value, 0, 0)
            state_b = _dot(query, grad * lead, 0, 0)
            if r < half:
                keeps[j][0, r] = state_a
                keeps[j][1, r] = state_b
            else:
                sends[2 * j][0, r - half] = state_a.astype(B16)
                sends[2 * j + 1][0, r - half] = state_b.astype(B16)


def _live(len_ref, first, n, scaling, later):
    t = lax.broadcasted_iota(jnp.int32, (n, n), later) + first
    s = lax.broadcasted_iota(jnp.int32, (n, n), 1 - later) + first
    begin = jnp.zeros((n, n), jnp.int32)
    total = jnp.int32(0)
    for k in range(len_ref.shape[0]):
        total = total + len_ref[k]
        begin = jnp.where(t >= total, total, begin)
    return jnp.where((s <= t) & (s >= begin), F32(scaling), F32(0.0))


def inner_kernel(scaling, place_ref, len_ref, head_ref, *refs):
    out = refs[-1]
    _, heads, n, d = head_ref.shape
    first = place_ref[0] * n
    down = _live(len_ref, first, n, scaling, 0)
    across = _live(len_ref, first, n, scaling, 1)
    for h in range(heads):
        query, key, value, grad = (head_ref[i, h] for i in range(4))
        ts = (_dot(grad, value, 1, 1) * down).astype(B16)
        st = (_dot(value, grad, 1, 1) * across).astype(B16)
        sc = (_dot(key, query, 1, 1) * across).astype(B16)
        out[0, h] = _dot(ts, key, 1, 0)
        out[1, h] = _dot(st, query, 1, 0)
        out[2, h] = _dot(sc, grad, 1, 0)


def grads_kernel(chunk, scaling, early, place_ref, len_ref, head_ref, mine_ref, *refs):
    got, outs, token_ref = refs[:4], refs[-11:-8], refs[-8]
    inner_ref = refs[4] if early else None
    wide, slabs, sems = refs[-7:-4], refs[-4:-1], refs[-1]
    token_ref[...] = jnp.zeros(token_ref.shape, token_ref.dtype)
    _, heads, n, d = head_ref.shape
    half = heads // 2
    first = place_ref[0] * n
    flip = place_ref[1]
    start, stop = _edges(len_ref, first, first + n - 1)
    row = lax.broadcasted_iota(jnp.int32, (n, d), 0) + first
    lead = jnp.where(row < stop, F32(1.0), F32(0.0))
    last = jnp.where(row >= start, F32(1.0), F32(0.0))
    last16 = last.astype(B16)
    cat = jnp.concatenate
    if not early:
        down = _live(len_ref, first, n, scaling, 0)
        across = _live(len_ref, first, n, scaling, 1)
    for r in range(heads):
        h = r ^ flip
        if r < half:
            state_a, state_b = mine_ref[0, r], mine_ref[1, r]
        else:
            side, o = divmod(r - half, half // 2)
            state_a, state_b = got[side][0, o], got[2 + side][0, o]
        query, key, value, grad = (head_ref[i, h] for i in range(4))
        at = pl.ds(h, n, stride=heads)
        if early:
            wide[0][at, :] = inner_ref[0, h] + _dot(grad, state_a, 1, 1) * lead
            wide[1][at, :] = inner_ref[1, h] + _dot(value, state_b, 1, 1) * last
            wide[2][at, :] = inner_ref[2, h] + _dot(key, state_b, 1, 0) * last
        else:
            x = _dot(grad, cat([value, state_a], axis=0), 1, 1)
            y = _dot(value, cat([grad, state_b], axis=0), 1, 1)
            z = _dot(key, query, 1, 1)
            ts = (x[:, :n] * down).astype(B16)
            st = (y[:, :n] * across).astype(B16)
            sc = (z * across).astype(B16)
            wide[0][at, :] = _dot(ts, key, 1, 0) + x[:, n:] * lead
            wide[1][at, :] = _dot(st, query, 1, 0) + y[:, n:] * last
            wide[2][at, :] = _dot(
                cat([sc, key * last16], axis=1), cat([grad, state_b], axis=0), 1, 0
            )
    copies = []
    for i, (scr, slab, out) in enumerate(zip(wide, slabs, outs)):
        slab[...] = scr[...].reshape(n, heads, d).astype(B16)
        copy = pltpu.make_async_copy(
            slab, out.at[:, pl.ds(chunk * heads, heads), :], sems.at[i]
        )
        copy.start()
        copies.append(copy)
    for copy in copies:
        copy.wait()


class Plan:
    def __init__(self, seq_size, head_size, n, heads, d, lengths):
        self.n, self.d, self.seq_size, self.head_size = n, d, seq_size, head_size
        self.head_bits, self.seq_bits = _log2(head_size), _log2(seq_size)
        self.levels = self.head_bits + self.seq_bits
        self.scaling = 1.0 / math.sqrt(d * (n * seq_size * head_size // 2))
        self.part = max(heads // CHUNKS, min(heads, head_size))
        self.chunks = heads // self.part
        self.total = heads
        self.lengths = lengths
        device = lax.axis_index("seq") * head_size + lax.axis_index("head")
        device = device.astype(jnp.int32)
        flip = sum(
            ((device >> level) & 1) * (self.part >> (level + 1))
            for level in range(self.head_bits)
        )
        self.place = jnp.stack([device, flip]).astype(jnp.int32)
        self.index, self.early = {}, {}
        for level in range(self.levels):
            names = ["up_own", "up_got"]
            if level < self.head_bits:
                names += ["m_in", "m_got", "s_in", "s_own"]
            else:
                names += ["unit"]
            for name in names + (["pick"] if level + 1 == self.levels else []):
                self.index[name, level] = len(self.index)

    def call(self, body, name, ins, in_specs, outs, out_specs, scratch, vmem=VMEM, cost=700, **kw):
        return pl.pallas_call(
            body,
            in_specs=in_specs,
            out_specs=out_specs,
            out_shape=outs,
            scratch_shapes=scratch,
            compiler_params=pltpu.CompilerParams(vmem_limit_bytes=vmem),
            cost_estimate=pl.CostEstimate(
                flops=1, bytes_accessed=int(cost * COST), transcendentals=0
            ),
            name=name,
            **kw,
        )(*ins)

    def states(self, chunks, arrays, after):
        n, d, part, count = self.n, self.d, self.part, len(chunks)
        shape = (2, part // 2, d, d)
        first = chunks[0] == 0
        outs = [jax.ShapeDtypeStruct(shape, F32)] * count
        outs += [jax.ShapeDtypeStruct((4, part, n, d), B16)] * count
        outs += [jax.ShapeDtypeStruct((1, *shape[1:]), B16)] * (2 * count)
        specs = [IN_VMEM] * len(outs)
        if first:
            outs = [jax.ShapeDtypeStruct((2 * len(self.index),), F32)] + outs
            specs = [IN_SMEM] + specs
        got = self.call(
            functools.partial(states_kernel, chunks, self.weights if first else None),
            "states",
            [self.place, self.lengths, *arrays, *after],
            [IN_SMEM] * 2 + [IN_HBM] * 4 + [ANYWHERE] * len(after),
            tuple(outs),
            specs,
            [pltpu.VMEM((count, 4, n, part, d), B16)]
            + [pltpu.VMEM((n * part, d), F32)] * 2
            + [pltpu.SemaphoreType.DMA((count, 4))],
            VMEM_FIRST if first else VMEM_NEXT,
            3500 * count,
        )
        if first:
            self.scalars, *got = got
        moved = [self.swap(x, 0) for x in got[2 * count :]]
        return got[:count], got[count : 2 * count], moved

    def inner(self, heads, after):
        return self.call(
            functools.partial(inner_kernel, self.scaling),
            "inner",
            [self.place, self.lengths, heads, *after],
            [IN_SMEM] * 2 + [IN_VMEM] + [ANYWHERE] * len(after),
            jax.ShapeDtypeStruct((3, self.part, self.n, self.d), F32),
            IN_VMEM,
            [],
        )

    def grads(self, chunk, heads, mine, got, inner, before, after):
        n, d, part = self.n, self.d, self.part
        out = jax.ShapeDtypeStruct((n, self.total, d), B16)
        return self.call(
            functools.partial(grads_kernel, chunk, self.scaling, len(inner) > 0),
            "grads",
            [self.place, self.lengths, heads, mine, *got, *inner, *before, *after],
            [IN_SMEM] * 2
            + [IN_VMEM] * (6 + len(inner))
            + [IN_HBM] * len(before)
            + [ANYWHERE] * len(after),
            (out, out, out, jax.ShapeDtypeStruct((8, 128), F32)),
            [IN_HBM] * 3 + [IN_VMEM],
            [pltpu.VMEM((n * part, d), F32)] * 3
            + [pltpu.VMEM((n, part, d), B16)] * 3
            + [pltpu.SemaphoreType.DMA((3,))],
            input_output_aliases={8 + len(inner) + i: i for i in range(len(before))},
        )

    def weights(self, place_ref, len_ref, out):
        n, bits = self.n, self.head_bits
        device = place_ref[0]
        begin = ((device >> bits) << bits) * n
        end = begin + (n << bits)
        pairs = []
        for level in range(self.levels):
            group = (device >> (level + 1)) << (level + 1)
            low, high = group * n, (group + (2 << level)) * n
            middle = (group + (1 << level)) * n
            pairs += [(middle - 1, high - 1), (low, middle)]
            if level < bits:
                pairs += [(middle - 1, middle)]
            else:
                pairs += [(middle - 1, begin), (end - 1, middle)]
        same = _same(len_ref, pairs)
        one, zero = F32(1.0), F32(0.0)

        def put(name, level, a, b):
            out[2 * self.index[name, level]] = a
            out[2 * self.index[name, level] + 1] = b

        for level in range(self.levels):
            hi = (device >> level) & 1 == 1
            lasts, firsts = same[0], same[1]
            put("up_own", level, jnp.where(hi, one, lasts), jnp.where(hi, firsts, one))
            put("up_got", level, jnp.where(hi, lasts, one), jnp.where(hi, one, firsts))
            if level < bits:
                join = same[2]
                same = same[3:]
                put("m_in", level, jnp.where(hi, firsts, one), jnp.where(hi, one, lasts))
                put("m_got", level, jnp.where(hi, join, zero), jnp.where(hi, zero, join))
                put("s_in", level, jnp.where(hi, one, firsts), jnp.where(hi, lasts, one))
                put("s_own", level, jnp.where(hi, zero, join), jnp.where(hi, join, zero))
            else:
                ahead, behind = same[2], same[3]
                same = same[4:]
                put("unit", level, jnp.where(hi, ahead, zero), jnp.where(hi, zero, behind))
            if level + 1 == self.levels:
                put("pick", level, jnp.where(hi, zero, one), jnp.where(hi, one, zero))


    def combine(self, name, body, ins, outs, after):
        def kernel(scalar_ref, *refs):
            body(
                lambda name, level, which: scalar_ref[2 * self.index[name, level] + which],
                refs[: len(ins)],
                refs[len(refs) - len(outs) :],
            )

        return self.call(
            kernel,
            name,
            [self.scalars, *ins, *after],
            [IN_SMEM] + [IN_VMEM] * len(ins) + [ANYWHERE] * len(after),
            tuple(outs),
            [IN_VMEM] * len(outs),
            [],
        )

    def order(self, count):
        chunks, size = self.chunks, max(1, self.chunks // 2)
        line = [(chunk, 1) for chunk in range(size)]
        line += [(chunk, 0) for chunk in range(size, chunks)]
        for wave in range(count - 2 + chunks - 1):
            for chunk in reversed(range(chunks)):
                one = (chunk, wave - chunk)
                if 0 < one[1] < count - 2 and one not in line:
                    line.append(one)
        fill, final = count - 2, count - 1
        spare = line[-2:] if chunks > 1 else []
        line = line[: len(line) - len(spare)]
        line += [(0, fill), *spare[:-1], (0, final)]
        if chunks > 2:
            line += [(2, -1)]
            line.insert(len(line) - 6, (1, -1))
            line.insert(1, (0, -1))
        line += spare[-1:]
        for chunk in range(1, chunks):
            line += [(chunk, fill)] if chunk == 1 else []
            line += [(chunk + 1, fill)] if chunk + 1 < chunks else []
            line.append((chunk, final))
        return line

    def swap(self, x, level):
        if level < self.head_bits:
            moves = [(i, i ^ (1 << level)) for i in range(self.head_size)]
            return lax.ppermute(x, "head", moves)
        bit = 1 << (level - self.head_bits)
        return lax.ppermute(x, "seq", [(i, i ^ bit) for i in range(self.seq_size)])

    def stages(self, chunk, keep, tokens, swapped):
        d, bits, last = self.d, self.head_bits, self.levels - 1
        own, got, here = [], [], {}

        def shaped(heads, dtype, lead=2):
            return jax.ShapeDtypeStruct((lead, heads, d, d), dtype)

        own.append(keep)
        here["heads"], here["got"] = tokens, swapped

        def up(level, after):
            got.append(here["got"] if level == 0 else [here["got"]])
            heads = own[-1].shape[1]
            half = heads // 2 if level + 1 < bits else heads

            def body(w, ins, outs):
                for which in range(2):
                    o, g = w("up_own", level, which), w("up_got", level, which)
                    for h in range(heads):
                        other = ins[1][which, h] if level else ins[1 + which][0, h]
                        x = o * ins[0][which, h] + g * other.astype(F32)
                        if h < half:
                            outs[0][which, h] = x
                        if half == heads:
                            outs[1][which, h] = x.astype(B16)
                        elif h >= half:
                            outs[1][which, h - half] = x.astype(B16)

            outs = [shaped(half, F32), shaped(half, B16)]
            keep, send = self.combine("up", body, [own[-1], *got[-1]], outs, after)
            if half < heads:
                own.append(keep)
            else:
                here["total"] = keep
            here["got"] = self.swap(send, level + 1)
            return keep

        def across(level, after):
            ins = [here["total"], here["got"]]
            if "state" in here:
                ins.append(here["state"])
            heads = ins[0].shape[1]
            final = level + 1 == last

            def body(w, ins, outs):
                for h in range(heads):
                    totals = []
                    for which in range(2):
                        other = ins[1][which, h].astype(F32)
                        x = w("up_own", level, which) * ins[0][which, h]
                        x = x + w("up_got", level, which) * other
                        y = w("unit", level, which) * other
                        if len(ins) > 2:
                            y = y + ins[2][which, h]
                        outs[0][which, h] = y
                        totals.append(x)
                        if not final:
                            outs[1][which, h] = x.astype(B16)
                            outs[2][which, h] = x
                    if final:
                        x = w("pick", last, 0) * totals[0] + w("pick", last, 1) * totals[1]
                        outs[1][0, h] = x.astype(B16)

            outs = [shaped(heads, F32), shaped(heads, B16, 1 if final else 2)]
            if not final:
                outs.append(shaped(heads, F32))
            state, send, *total = self.combine("across", body, ins, outs, after)
            here["state"] = state
            here["total"] = total[0] if total else None
            here["got"] = self.swap(send, level + 1)
            return state

        def down(level, after):
            top = level == bits - 1
            ins = [here["state"], here["got"], own[level], *got[level]]
            heads = own[level].shape[1]
            half = heads // 2
            factor = self.scaling if level == 0 else 1.0

            def body(w, ins, outs):
                for which in range(2):
                    m_in, m_got, s_in, s_own = (
                        factor * w(name, level, which)
                        for name in ("m_in", "m_got", "s_in", "s_own")
                    )
                    for h in range(heads):
                        if top:
                            x = w("unit", last, which) * ins[1][0, h].astype(F32)
                            x = x + ins[0][which, h]
                        elif h < half:
                            x = ins[0][which, h]
                        else:
                            x = ins[1][which, h - half].astype(F32)
                        other = ins[3][which, h] if level else ins[3 + which][0, h]
                        mine = m_in * x + m_got * other.astype(F32)
                        theirs = s_in * x + s_own * ins[2][which, h]
                        outs[0][which, h] = mine.astype(outs[0].dtype)
                        if level:
                            outs[1][which, h] = theirs.astype(B16)
                        else:
                            outs[1 + 2 * which + h // half][0, h % half] = theirs.astype(B16)

            if level:
                outs = [shaped(heads, F32), shaped(heads, B16)]
            else:
                outs = [shaped(heads, B16)] + [shaped(half, B16, 1)] * 4
            here["state"], *send = self.combine("down", body, ins, outs, after)
            moved = [self.swap(x, level) for x in send]
            here["got"] = moved if level == 0 else moved[0]
            return here["state"]

        def final(before, after):
            *outs, token = self.grads(
                chunk, here["heads"], here["state"], here["got"], here["inner"], before, after
            )
            return outs, token

        def early(after):
            here["inner"] = (self.inner(here["heads"], after),)
            return here["inner"][0]

        here["inner"] = ()
        self.early[chunk] = early
        steps = [functools.partial(up, level) for level in range(bits)]
        steps += [functools.partial(across, level) for level in range(bits, last)]
        steps += [functools.partial(down, level) for level in reversed(range(bits))]
        return steps + [final]


def local(seq_size, head_size, queries, key_heads, value_heads, grad_output, doc_lengths):
    n, heads, d = queries.shape
    arrays = (queries, key_heads, value_heads, grad_output)
    plan = Plan(seq_size, head_size, n, heads, d, doc_lengths)
    stages, after = [], ()
    size = max(1, plan.chunks // 2)
    for begin in range(0, plan.chunks, size):
        chunks = list(range(begin, begin + size))
        keeps, tokens, moved = plan.states(chunks, arrays, after)
        after = (keeps[0],)
        for spot, chunk in enumerate(chunks):
            swapped = moved[2 * spot : 2 * spot + 2]
            stages.append(plan.stages(chunk, keeps[spot], tokens[spot], swapped))
        if begin == 0:
            for chunk in chunks:
                after = (stages[chunk][0](after),)
    outs, count = (), len(stages[0])
    for chunk, stage in plan.order(count):
        if stage < 0:
            after = (plan.early[chunk](after),)
        elif stage + 1 < count:
            after = (stages[chunk][stage](after),)
        else:
            outs, token = stages[chunk][stage](outs, after)
            after = (token,)
    return tuple(outs)


def solution(mesh):
    placed = P(("seq", "head"), None, None)
    return jax.shard_map(
        functools.partial(local, mesh.shape["seq"], mesh.shape["head"]),
        mesh=mesh,
        in_specs=(placed, placed, placed, placed, P()),
        out_specs=(placed, placed, placed),
        check_vma=False,
    )
```
